1024 devices in a mesh: dp: 64 (over x, y), tensor: 8 (over z_hi, core), replica: 2 (over z_lo).
Axes of the slice: x: 8, y: 8, z: 8 (z_hi: 4, z_lo: 2; z = z_hi * 2 + z_lo), core: 2. Of those that a mesh axis runs over, the one named last changes fastest.
Arguments:
- tokens: bfloat16 [16384, 3072], P(('dp', 'replica')), may hold values from -6 to 6
- queries: bfloat16 [16384, 3072], P(('dp', 'replica'), 'tensor'), may hold values from -172 to 172
- key_rows: bfloat16 [16384, 3072], P(('dp', 'replica'), 'tensor'), may hold values from -4.5 to 4.5
- value_rows: bfloat16 [16384, 3072], P(('dp', 'replica'), 'tensor'), may hold values from -6 to 6
- cotangent: bfloat16 [16384, 3072], P(('dp', 'replica'), 'tensor'), may hold values from -0.23925781 to 0.23925781
- probe_shards: bfloat16 [8, 1327104], P('tensor', 'dp'), may hold values from -4 to 4
- hess_old: float32 [8, 1327104], P('tensor', 'dp'), may hold values from -1.5 to 1.5
- shard_counts: int32 [64], replicated, may hold values from 16128 to 20736, as said below
Outputs:
- hess_new: float32 [8, 1327104], P('tensor', 'dp')
The draws below stay inside these ranges and needn't reach their ends.
Inputs may be any that keep to these rules, and one draw needn't show every extreme that they name: `shard_counts`: every entry is a multiple of 128, the entries sum to 1179648, and the largest is exactly 20736; slots of a shard past its count are not read.
All inputs are finite; a program needn't handle non-finite values.
Results may differ from the reference program's by a relative error of at most 0.0035.
Values may be sent and summed in bfloat16 or wider, within the bound.
No kernel may reach another device: no remote copies, remote signals or barrier semaphores. Data moves between devices by JAX's collectives and lax.ppermute only.
A program may use at most 32 MiB of HBM per device.

```python
import math
import jax
import jax.numpy as jnp
from jax import lax

DW = 3072
HEAD = 96
TOK_DEV = 128
HEADS = 32
COLS = 384
TOKENS = 16384
CAP = 20736
N_DP = 64
N_TENSOR = 8


def pair_parts(key):
    sequences = TOKENS // TOK_DEV
    band = TOK_DEV // 8
    query_key, key_key, row_key, col_key, power_key, gap_key = jax.random.split(key, 6)
    full_shape = (sequences, TOK_DEV, HEADS, HEAD)
    base_queries = jnp.clip(jax.random.normal(query_key, full_shape, jnp.float32), -4.5, 4.5)
    base_keys = jnp.clip(jax.random.normal(key_key, full_shape, jnp.float32), -4.5, 4.5)
    offsets = jnp.arange(4, dtype=jnp.int32) * band
    target_rows = (TOK_DEV // 2 + offsets[None, :] + jax.random.randint(row_key, (sequences, 4), 0, band)).astype(jnp.int32)
    source_rows = (offsets[None, :] + 1 + jax.random.randint(col_key, (sequences, 4), 0, band - 1)).astype(jnp.int32)
    strengths = jax.random.uniform(power_key, (sequences, 4), jnp.float32, 10.0, 38.0)
    gaps = jax.random.uniform(gap_key, (sequences, 4), jnp.float32, 1.5, 2.5)
    return (base_queries, base_keys, target_rows, source_rows, strengths, gaps)


def draw_queries(key, part):
    parts = pair_parts(key)
    chosen = parts[0]
    return chosen.reshape(TOKENS, HEADS * HEAD).astype(jnp.bfloat16)


def draw_key_rows(key, part):
    parts = pair_parts(key)
    chosen = parts[1]
    return chosen.reshape(TOKENS, HEADS * HEAD).astype(jnp.bfloat16)


def draw_shard_counts(key, part):
    key = jax.random.fold_in(key, 11)
    total_blocks = DW * COLS // 128
    base = total_blocks // N_DP
    spread = max(2, base // 8)
    first_key, second_key = jax.random.split(key)
    order = jax.random.permutation(first_key, N_DP)
    shifts = jax.random.randint(second_key, (N_DP // 2,), 0, spread + 1).astype(jnp.int32)
    shifts = shifts.at[0].set(spread)
    amounts = jnp.concatenate([base + shifts, base - shifts]).astype(jnp.int32)
    blocks = jnp.zeros((N_DP,), jnp.int32).at[order].set(amounts)
    return (blocks * 128).astype(jnp.int32)


def shard_levels(stream_key, extent, shards, least, high):
    factor_of = 1.0
    for axis_at, blocks in shards:
        heights = jax.random.uniform(jax.random.fold_in(jax.random.fold_in(stream_key, 6), axis_at), (blocks,), jnp.float32, least / len(shards), high / len(shards))
        factor_of = factor_of * jnp.repeat(jnp.exp(heights), extent[axis_at] // blocks).reshape((-1,) + (1,) * (len(extent) - 1 - axis_at))
    return factor_of


def normal_values(key, dims, scale, most, cuts=(), kind=jnp.bfloat16):
    values = scale * jax.random.normal(key, dims, jnp.float32)
    if cuts:
        values = values * shard_levels(key, dims, cuts, -0.22, 0.18)
    return jnp.clip(values, -most, most).astype(kind)


def setup_inputs(seed: int = 0) -> dict:
    key_list = jax.random.split(jax.random.key(seed), 9)
    tokens = normal_values(key_list[0], (TOKENS, DW), 1.0, 6.0, ((0, 128),))
    queries = draw_queries(jax.random.fold_in(key_list[8], 71), 0)
    key_rows = draw_key_rows(jax.random.fold_in(key_list[8], 71), 0)
    value_rows = normal_values(key_list[3], (TOKENS, HEADS * HEAD), 1.0, 6.0, ((0, 128), (1, 8)))
    cotangent = normal_values(key_list[4], (TOKENS, HEADS * HEAD), 0.04, 0.23925781, ((0, 128), (1, 8)))
    probe_shards = normal_values(key_list[5], (N_TENSOR, N_DP * CAP), 1.0, 4.0, ((0, 8), (1, 64)))
    hess_old = normal_values(key_list[6], (N_TENSOR, N_DP * CAP), 0.3, 1.5, ((0, 8), (1, 64)), jnp.float32)
    shard_counts = draw_shard_counts(jax.random.fold_in(key_list[8], 71), 0)
    return {"tokens": tokens, "queries": queries, "key_rows": key_rows, "value_rows": value_rows, "cotangent": cotangent, "probe_shards": probe_shards, "hess_old": hess_old, "shard_counts": shard_counts}


decay_rate = 0.99

def shard_tables(counts):
    block_sizes = (counts // 128).astype(jnp.int32)
    starts = (jnp.cumsum(block_sizes) - block_sizes).astype(jnp.int32)
    return (block_sizes, starts)

def spread_probe(gathered, block_sizes, starts, cap_blocks, total_blocks, width, columns):
    inner_slot = lax.iota(jnp.int32, cap_blocks)
    in_use = inner_slot[None, :] < block_sizes[:, None]
    target = jnp.where(in_use, starts[:, None] + inner_slot[None, :], total_blocks).astype(jnp.int32).reshape(-1)
    slab_blocks = jnp.zeros((total_blocks, 128), gathered.dtype).at[target].set(gathered.reshape(-1, 128), mode='drop')
    return slab_blocks.reshape(width, columns)

def pick_slots(hessian_blocks, block_sizes, starts, first_slot, slot_count):
    inner_slot = (first_slot + lax.iota(jnp.int32, slot_count)).astype(jnp.int32)
    in_use = inner_slot[None, :] < block_sizes[:, None]
    source = jnp.where(in_use, starts[:, None] + inner_slot[None, :], 0).astype(jnp.int32)
    return jnp.where(in_use[:, :, None], hessian_blocks[source], jnp.float32(0.0))

def second_order(query, key_head, value_head, cot_head, tangent_head):
    inv_root = 1.0 / math.sqrt(query.shape[1])
    length = query.shape[0]
    scores = inv_root * jnp.dot(query, key_head.T, preferred_element_type=jnp.float32)
    causal = lax.iota(jnp.int32, length)[:, None] >= lax.iota(jnp.int32, length)[None, :]
    scores = jnp.where(causal, scores, jnp.float32(-1e+30))
    row_peak = lax.optimization_barrier(jnp.max(scores, axis=1, keepdims=True))
    expo_terms = jnp.exp(scores - row_peak)
    attn_weights = expo_terms / lax.optimization_barrier(jnp.sum(expo_terms, axis=1, keepdims=True))
    score_tangent = inv_root * jnp.dot(tangent_head, key_head.T, preferred_element_type=jnp.float32)
    back_scores = jnp.dot(cot_head, value_head.T, preferred_element_type=jnp.float32)
    row_delta = lax.optimization_barrier(jnp.sum(attn_weights * back_scores, axis=1, keepdims=True))
    mean_tangent = lax.optimization_barrier(jnp.sum(attn_weights * score_tangent, axis=1, keepdims=True))
    weight_tangent = attn_weights * (score_tangent - mean_tangent)
    delta_tangent = lax.optimization_barrier(jnp.sum(weight_tangent * back_scores, axis=1, keepdims=True))
    grad_tangent = (weight_tangent * (back_scores - row_delta) - attn_weights * delta_tangent).astype(jnp.bfloat16)
    return (inv_root * jnp.dot(grad_tangent, key_head, preferred_element_type=jnp.float32)).astype(jnp.bfloat16)

def head_rows(query, key_part, value_part, cot_part, tangent_part, head_size):
    length, columns = query.shape

    def by_head(array):
        return array.reshape(length, columns // head_size, head_size).transpose(1, 0, 2)
    result = lax.map(lambda bundle: second_order(*bundle), (by_head(query), by_head(key_part), by_head(value_part), by_head(cot_part), by_head(tangent_part)))
    return result.transpose(1, 0, 2).reshape(length, columns)

def reference(tokens, queries, key_rows, value_rows, cotangent, probe_shards, hess_old, shard_counts):
    cap_blocks = CAP // 128
    total_blocks = DW * COLS // 128
    block_sizes, starts = shard_tables(shard_counts)
    sequences = TOKENS // TOK_DEV
    group_rows = 2 * TOK_DEV
    groups = TOKENS // group_rows
    outputs = []
    for tensor_rank in range(N_TENSOR):
        probe_full = spread_probe(probe_shards[tensor_rank], block_sizes, starts, cap_blocks, total_blocks, DW, COLS)
        tangent = jnp.dot(tokens, probe_full, preferred_element_type=jnp.float32).astype(jnp.bfloat16)
        low = tensor_rank * COLS
        pieces = tuple((array.reshape(sequences, TOK_DEV, COLS) for array in (queries[:, low:low + COLS], key_rows[:, low:low + COLS], value_rows[:, low:low + COLS], cotangent[:, low:low + COLS], tangent)))
        scaled = lax.map(lambda bundle: head_rows(*bundle, HEAD), pieces).reshape(TOKENS, COLS)

        def add_group(total, group_index):
            start = (group_index * group_rows).astype(jnp.int32)
            token_part = lax.dynamic_slice_in_dim(tokens, start, group_rows, 0)
            scaled_part = lax.dynamic_slice_in_dim(scaled, start, group_rows, 0)
            term = jnp.dot(token_part.T, scaled_part, preferred_element_type=jnp.float32).astype(jnp.bfloat16)
            term = lax.optimization_barrier(term)
            return (total + term.astype(jnp.float32), None)
        hessian_probe, _ = lax.scan(add_group, jnp.zeros((DW, COLS), jnp.float32), jnp.arange(groups, dtype=jnp.int32))
        padded = pick_slots(hessian_probe.reshape(-1, 128), block_sizes, starts, jnp.int32(0), cap_blocks).reshape(-1)
        outputs.append(decay_rate * hess_old[tensor_rank] + (1.0 - decay_rate) * probe_shards[tensor_rank].astype(jnp.float32) * padded)
    return jnp.stack(outputs)
```

```python
import math

import jax
import jax.numpy as jnp
from jax import lax
from jax.experimental import pallas as pl
from jax.experimental.pallas import tpu as pltpu
from jax.sharding import PartitionSpec as P

HEAD = 96
LANES = 128
HALF = LANES // 2
decay_rate = 0.99

BLOCKS = 3
OUTER = 56
PAIRED = 32
WINDOW = OUTER + PAIRED

VMEM = pl.BlockSpec(memory_space=pltpu.VMEM)
SMEM = pl.BlockSpec(memory_space=pltpu.SMEM)


def params():
    return pltpu.CompilerParams(vmem_limit_bytes=48 * 1024 * 1024)


def left_lanes(rows):
    return lax.broadcasted_iota(jnp.int32, (rows, LANES), 1) < HALF


def first_block(counts_ref, shard):
    return lax.fori_loop(0, shard, lambda at, total: total + counts_ref[at] // LANES, jnp.int32(0))


def pack_shard(place_ref, counts_ref, probe_ref, out_ref, rows):
    copy = place_ref[0]
    shift = lax.rem(first_block(counts_ref, place_ref[1]), BLOCKS)
    rows[...] = jnp.zeros_like(rows)
    for block in range(probe_ref.shape[1] // LANES):
        rows[pl.ds(shift + block, 1), :] = probe_ref[0:1, block * LANES : (block + 1) * LANES].astype(jnp.float32)
    outer = rows[pl.ds(2 * copy, OUTER, stride=BLOCKS), :]
    middle = rows[pl.ds(1, OUTER, stride=BLOCKS), :]
    turned = pltpu.roll(middle, HALF, 1)
    near = jnp.where(copy == 0, middle, turned)
    far = jnp.where(copy == 0, turned, middle)
    far = jnp.concatenate([far[PAIRED:], jnp.zeros((2 * PAIRED - OUTER, LANES), jnp.float32)], axis=0)
    paired = jnp.where(left_lanes(PAIRED), near[:PAIRED], far)
    window = jnp.concatenate([outer, paired], axis=0).astype(jnp.bfloat16)

    def store(shard, carry):
        out_ref[shard] = window
        return carry

    lax.fori_loop(0, out_ref.shape[0], store, 0, unroll=8)


def split_heads(place_ref, query_ref, key_ref, value_ref, cot_ref, keep_ref, send_ref):
    copy = place_ref[0]
    width = query_ref.shape[1] // 2

    def fill(first_ref, second_ref):
        for at, ref in enumerate((query_ref, key_ref, value_ref, cot_ref)):
            first_ref[:, at * width : (at + 1) * width] = ref[:, :width]
            second_ref[:, at * width : (at + 1) * width] = ref[:, width:]

    @pl.when(copy == 0)
    def _():
        fill(keep_ref, send_ref)

    @pl.when(copy == 1)
    def _():
        fill(send_ref, keep_ref)


def transpose_tokens(own_ref, other_ref, out_ref):
    length = own_ref.shape[0]
    out_ref[:, :length] = own_ref[...].T
    out_ref[:, length:] = other_ref[...].T


def second_order(query, key_head, value_head, cot_head, tangent):
    length = query.shape[0]
    inv_root = 1.0 / math.sqrt(HEAD)
    causal = lax.broadcasted_iota(jnp.int32, (length, length), 0) >= lax.broadcasted_iota(
        jnp.int32, (length, length), 1
    )

    def times_transposed(left, right):
        return lax.dot_general(left, right, (((1,), (1,)), ((), ())), preferred_element_type=jnp.float32)

    scores = inv_root * times_transposed(query, key_head)
    scores = jnp.where(causal, scores, jnp.float32(-1e30))
    expo_terms = jnp.exp(scores - jnp.max(scores, axis=1, keepdims=True))
    attn = expo_terms / jnp.sum(expo_terms, axis=1, keepdims=True)
    score_tangent = inv_root * times_transposed(tangent, key_head)
    back = times_transposed(cot_head, value_head)
    delta = jnp.sum(attn * back, axis=1, keepdims=True)
    mean_tangent = jnp.sum(attn * score_tangent, axis=1, keepdims=True)
    weight_tangent = attn * (score_tangent - mean_tangent)
    delta_tangent = jnp.sum(weight_tangent * back, axis=1, keepdims=True)
    grad_tangent = (weight_tangent * (back - delta) - attn * delta_tangent).astype(jnp.bfloat16)
    return (inv_root * jnp.dot(grad_tangent, key_head, preferred_element_type=jnp.float32)).astype(jnp.bfloat16)


def middle_part(
    place_ref,
    counts_ref,
    pieces_ref,
    own_tokens_ref,
    other_tokens_ref,
    turned_ref,
    own_heads_ref,
    other_heads_ref,
    out_ref,
    outer,
    middle,
    probe,
    tangent,
    scaled,
    spread,
):
    copy = place_ref[0]
    length, features = own_tokens_ref.shape
    shards = pieces_ref.shape[0]
    columns = tangent.shape[1]
    left = left_lanes(PAIRED)
    top_row = lax.broadcasted_iota(jnp.int32, (8, LANES), 0) == 0

    def place(shard, start):
        first = start // BLOCKS
        shift = start - first * BLOCKS
        piece = pieces_ref[shard].astype(jnp.float32)
        paired = piece[OUTER:]
        for slab, block, values in (
            (outer, 2 * copy, piece[:OUTER]),
            (
                middle,
                1,
                jnp.concatenate(
                    [jnp.where(left, paired, 0.0), jnp.where(left, 0.0, paired)[: OUTER - PAIRED]], axis=0
                ),
            ),
        ):
            before = slab[pl.ds(first, 8), :]
            slab[pl.ds(first, 8), :] = jnp.where(top_row & (block < shift), before, values[:8])
            slab[pl.ds(first + 8, OUTER - 8), :] = values[8:]
        return start + counts_ref[shard] // LANES

    lax.fori_loop(0, shards, place, jnp.int32(0), unroll=4)
    probe[:, :LANES] = outer[:features, :].astype(jnp.bfloat16)
    probe[:, LANES:] = middle[:features, :].astype(jnp.bfloat16)

    for at, tokens_ref in enumerate((own_tokens_ref, other_tokens_ref)):
        product = jnp.dot(tokens_ref[...], probe[...], preferred_element_type=jnp.float32)
        rows = slice(at * length, (at + 1) * length)
        outer_part = product[:, :LANES].astype(jnp.bfloat16)
        middle_half = (product[:, LANES : LANES + HALF] + product[:, LANES + HALF :]).astype(jnp.bfloat16)

        @pl.when(copy == 0)
        def _():
            tangent[rows, :LANES] = outer_part
            tangent[rows, LANES:] = middle_half

        @pl.when(copy == 1)
        def _():
            tangent[rows, :HALF] = middle_half
            tangent[rows, HALF:] = outer_part

    for at, heads_ref in enumerate((own_heads_ref, other_heads_ref)):
        rows = slice(at * length, (at + 1) * length)
        for head in range(columns // HEAD):
            cuts = [slice(part * columns + head * HEAD, part * columns + (head + 1) * HEAD) for part in range(4)]
            cut = slice(head * HEAD, (head + 1) * HEAD)
            scaled[rows, cut] = second_order(*(heads_ref[:, one] for one in cuts), tangent[rows, cut])

    @pl.when(copy == 0)
    def _():
        spread[:, :LANES] = scaled[:, :LANES]
        spread[:, LANES : LANES + HALF] = scaled[:, LANES:]
        spread[:, LANES + HALF :] = scaled[:, LANES:]

    @pl.when(copy == 1)
    def _():
        spread[:, :LANES] = scaled[:, HALF:]
        spread[:, LANES : LANES + HALF] = scaled[:, :HALF]
        spread[:, LANES + HALF :] = scaled[:, :HALF]

    term = jnp.dot(turned_ref[...], spread[...], preferred_element_type=jnp.float32)
    outer[:features, :] = term[:, :LANES]
    middle[:features, :] = term[:, LANES:]

    def cut_out(shard, start):
        first = start // BLOCKS
        paired = jnp.where(left, middle[pl.ds(first, PAIRED), :], middle[pl.ds(first + PAIRED, PAIRED), :])
        out_ref[shard] = jnp.concatenate([outer[pl.ds(first, OUTER), :], paired], axis=0).astype(jnp.bfloat16)
        return start + counts_ref[shard] // LANES

    lax.fori_loop(0, shards, cut_out, jnp.int32(0), unroll=4)


def add_groups(terms_ref, out_ref):
    def add(group, total):
        return total + terms_ref[group].astype(jnp.float32)

    out_ref[...] = lax.fori_loop(0, terms_ref.shape[0], add, jnp.zeros(out_ref.shape, jnp.float32), unroll=4)


def update_shard(place_ref, counts_ref, own_ref, other_ref, probe_ref, hess_ref, out_ref, rows):
    copy = place_ref[0]
    shard = place_ref[1]
    shift = lax.rem(first_block(counts_ref, shard), BLOCKS)
    blocks = probe_ref.shape[0]
    first = jnp.where(copy == 0, own_ref[...], other_ref[...])
    second = jnp.where(copy == 0, other_ref[...], own_ref[...])
    left = left_lanes(PAIRED)
    low, high = first[OUTER:], second[OUTER:]
    near = jnp.where(left, low, pltpu.roll(high, HALF, 1))
    far = jnp.where(left, pltpu.roll(low, HALF, 1), high)
    rows[pl.ds(0, OUTER, stride=BLOCKS), :] = first[:OUTER]
    rows[pl.ds(1, OUTER, stride=BLOCKS), :] = jnp.concatenate([near, far[: OUTER - PAIRED]], axis=0)
    rows[pl.ds(2, OUTER, stride=BLOCKS), :] = second[:OUTER]
    inner = lax.broadcasted_iota(jnp.int32, (blocks, LANES), 0)
    product = jnp.where(inner < counts_ref[shard] // LANES, rows[pl.ds(shift, blocks), :], 0.0)
    out_ref[...] = decay_rate * hess_ref[...] + (1.0 - decay_rate) * probe_ref[...].astype(jnp.float32) * product


def call(kernel, shape, dtype, operands, scalars, scratch=()):
    return pl.pallas_call(
        kernel,
        out_shape=jax.ShapeDtypeStruct(shape, dtype) if isinstance(shape, tuple) else shape,
        in_specs=[SMEM] * scalars + [VMEM] * (len(operands) - scalars),
        out_specs=VMEM if isinstance(shape, tuple) else [VMEM] * len(shape),
        scratch_shapes=list(scratch),
        compiler_params=params(),
        name=kernel.__name__,
    )(*operands)


def body(tokens, queries, key_rows, value_rows, cotangent, probe_shards, hess_old, shard_counts):
    length, width = tokens.shape
    half = queries.shape[1] // 2
    shards = shard_counts.shape[0]
    blocks = probe_shards.shape[1] // LANES
    slab = pltpu.VMEM((width + 2 * PAIRED, LANES), jnp.float32)
    rows = pltpu.VMEM((BLOCKS * OUTER + 8, LANES), jnp.float32)
    place = jnp.stack([lax.axis_index("replica"), lax.axis_index("dp")]).astype(jnp.int32)
    swap = [(0, 1), (1, 0)]

    packed = call(
        pack_shard, (shards, WINDOW, LANES), jnp.bfloat16, (place, shard_counts, probe_shards), 2, (rows,)
    )
    pieces = lax.all_to_all(packed, "dp", 0, 0)

    other_tokens = lax.ppermute(tokens, "replica", swap)
    both = jax.ShapeDtypeStruct((length, 4 * half), jnp.bfloat16)
    own_heads, sent_heads = call(
        split_heads, [both, both], None, (place, queries, key_rows, value_rows, cotangent), 1
    )
    other_heads = lax.ppermute(sent_heads, "replica", swap)
    turned = call(transpose_tokens, (width, 2 * length), jnp.bfloat16, (tokens, other_tokens), 0)

    windows = call(
        middle_part,
        (shards, WINDOW, LANES),
        jnp.bfloat16,
        (place, shard_counts, pieces, tokens, other_tokens, turned, own_heads, other_heads),
        2,
        (
            slab,
            slab,
            pltpu.VMEM((width, 2 * LANES), jnp.bfloat16),
            pltpu.VMEM((2 * length, half), jnp.bfloat16),
            pltpu.VMEM((2 * length, half), jnp.bfloat16),
            pltpu.VMEM((2 * length, 2 * LANES), jnp.bfloat16),
        ),
    )
    terms = lax.all_to_all(windows, "dp", 0, 0)
    summed = call(add_groups, (WINDOW, LANES), jnp.float32, (terms,), 0)
    other_summed = lax.ppermute(summed, "replica", swap)
    updated = call(
        update_shard,
        (blocks, LANES),
        jnp.float32,
        (
            place,
            shard_counts,
            summed,
            other_summed,
            probe_shards.reshape(blocks, LANES),
            hess_old.reshape(blocks, LANES),
        ),
        2,
        (rows,),
    )
    return updated.reshape(1, blocks * LANES)


def solution(mesh):
    placed = (
        P(("dp", "replica"), None),
        P(("dp", "replica"), "tensor"),
        P(("dp", "replica"), "tensor"),
        P(("dp", "replica"), "tensor"),
        P(("dp", "replica"), "tensor"),
        P("tensor", "dp"),
        P("tensor", "dp"),
        P(),
    )
    return jax.shard_map(
        body, mesh=mesh, in_specs=placed, out_specs=P("tensor", "dp"), check_vma=False
    )
```

```python
import math

import jax
import jax.numpy as jnp
from jax import lax
from jax.experimental import pallas as pl
from jax.experimental.pallas import tpu as pltpu
from jax.sharding import PartitionSpec as P

HEAD = 96
LANES = 128
decay_rate = 0.99

ROW = 8

HEADS = 4

BLOCKS = 3
WIDE = ((0, 0), (1, 0), (1, 64), (2, 64))
SLIM = ((0, 64), (0, 96), (2, 0), (2, 32))
SPAN = 64
PAIRS = SPAN // 2
QUADS = SPAN // 4
WINDOW = PAIRS + QUADS
USED = 56
HALF = LANES // 2
QUARTER = LANES // 4

VMEM = pl.BlockSpec(memory_space=pltpu.VMEM)
SMEM = pl.BlockSpec(memory_space=pltpu.SMEM)


def params():
    return pltpu.CompilerParams(vmem_limit_bytes=56 * 1024 * 1024)


def lane_of(rows):
    return lax.broadcasted_iota(jnp.int32, (rows, LANES), 1)


def turn(values, lanes):
    lanes = lanes % LANES
    return values if lanes == 0 else pltpu.roll(values, lanes, 1)


def first_block(counts_ref, shard):
    return lax.fori_loop(0, shard, lambda at, total: total + counts_ref[at] // LANES, jnp.int32(0))


def by_quarter(parts):
    lane = lane_of(parts[0].shape[0])
    low = jnp.where(lane < QUARTER, parts[0], parts[1])
    high = jnp.where(lane < 3 * QUARTER, parts[2], parts[3])
    return jnp.where(lane < HALF, low, high)


def pack_shard(place_ref, counts_ref, probe_ref, out_ref, rows):
    copy = place_ref[0]
    shift = lax.rem(first_block(counts_ref, place_ref[1]), BLOCKS)
    rows[...] = jnp.zeros_like(rows)
    for block in range(probe_ref.shape[1] // LANES):
        rows[pl.ds(shift + block, 1), :] = probe_ref[0:1, block * LANES : (block + 1) * LANES].astype(jnp.float32)

    def window(head):
        block, lane = WIDE[head]
        wide = rows[pl.ds(block, SPAN, stride=BLOCKS), :]
        pairs = jnp.where(lane_of(PAIRS) < HALF, turn(wide[:PAIRS], -lane), turn(wide[PAIRS:], HALF - lane))
        block, lane = SLIM[head]
        slim = rows[pl.ds(block, SPAN, stride=BLOCKS), :]
        quads = by_quarter(
            [turn(slim[at * QUADS : (at + 1) * QUADS], at * QUARTER - lane) for at in range(4)]
        )
        return jnp.concatenate([pairs, quads], axis=0).astype(jnp.bfloat16)

    for which in range(2):

        @pl.when(copy == which)
        def _():
            even, odd = window(2 * which), window(2 * which + 1)

            def store(at, carry):
                first = at // ROW * 2 * ROW + lax.rem(at, ROW)
                out_ref[first] = even
                out_ref[first + ROW] = odd
                return carry

            lax.fori_loop(0, out_ref.shape[0] // 2, store, 0, unroll=4)


def split_heads(place_ref, tokens_ref, query_ref, key_ref, value_ref, cot_ref, keep_ref, x_ref, copy_ref):
    copy, parity, core = place_ref[0], place_ref[2], place_ref[3]
    length, features = tokens_ref.shape
    half = length // 2
    packed = 2 * HEADS * HEAD
    tokens = tokens_ref[pl.ds(pl.multiple_of(core * half, half), half), :]
    x_ref[:, packed : packed + features] = tokens
    copy_ref[:, :features] = tokens
    arrays = (query_ref, key_ref, value_ref, cot_ref)

    def put(head, target_ref, start):
        for side in range(2):
            for at, ref in enumerate(arrays):
                to = start + (side * HEADS + at) * HEAD
                target_ref[:, to : to + HEAD] = ref[side * half : (side + 1) * half, head * HEAD : (head + 1) * HEAD]

    for mine in range(HEADS):

        @pl.when(2 * copy + parity == mine)
        def _():
            for at, ref in enumerate(arrays):
                keep_ref[:, at * HEAD : (at + 1) * HEAD] = ref[:, mine * HEAD : (mine + 1) * HEAD]
            put(mine ^ 1, x_ref, 0)
            put(mine ^ 3, x_ref, packed + features)
            put(mine ^ 2, copy_ref, features)


def attention_part(heads):
    length = heads.shape[0]
    query, key_head, value_head, cot_head = (heads[:, at * HEAD : (at + 1) * HEAD] for at in range(HEADS))
    inv_root = 1.0 / math.sqrt(HEAD)
    causal = lax.broadcasted_iota(jnp.int32, (length, length), 0) >= lax.broadcasted_iota(
        jnp.int32, (length, length), 1
    )
    scores = inv_root * times_transposed(query, key_head)
    scores = jnp.where(causal, scores, jnp.float32(-1e30))
    expo_terms = jnp.exp(scores - jnp.max(scores, axis=1, keepdims=True))
    attn = expo_terms / jnp.sum(expo_terms, axis=1, keepdims=True)
    back = times_transposed(cot_head, value_head)
    return key_head, attn, back, back - jnp.sum(attn * back, axis=1, keepdims=True)


def times_transposed(left, right):
    return lax.dot_general(left, right, (((1,), (1,)), ((), ())), preferred_element_type=jnp.float32)


def gather_sequences(features, place_ref, whole, halves, out_refs):
    core = place_ref[3]
    tokens_ref, turned_ref, key_ref, attn_ref, back_ref, centred_ref = out_refs
    length = attn_ref.shape[1]
    half = length // 2
    packed = 2 * HEADS * HEAD
    at = 0
    heads_of = []
    for one_ref, heads_ref in whole:
        tokens_ref[at * length : (at + 1) * length, :] = one_ref[...]
        heads_of.append(heads_ref[...])
        at += 1
    for mine_ref, mine_at, heads_at, other_ref, other_row in halves:
        tokens_ref[pl.ds(pl.multiple_of(at * length + core * half, half), half), :] = mine_ref[
            :, mine_at : mine_at + features
        ]
        tokens_ref[pl.ds(pl.multiple_of(at * length + (1 - core) * half, half), half), :] = other_ref[
            other_row : other_row + half, :
        ]
        heads_of.append(
            jnp.concatenate(
                [
                    mine_ref[:, heads_at : heads_at + packed // 2],
                    mine_ref[:, heads_at + packed // 2 : heads_at + packed],
                ],
                axis=0,
            )
        )
        at += 1
    for at, heads in enumerate(heads_of):
        rows = slice(at * length, (at + 1) * length)
        turned_ref[:, rows] = tokens_ref[rows, :].T
        key_ref[at], attn_ref[at], back_ref[at], centred_ref[at] = attention_part(heads)


def gather_three(place_ref, tokens_ref, keep_ref, x_ref, copy_ref, swapped_ref, *out_refs):
    features = tokens_ref.shape[1]
    packed = 2 * HEADS * HEAD
    gather_sequences(
        features,
        place_ref,
        [(tokens_ref, keep_ref)],
        [
            (x_ref, packed, 0, swapped_ref, 0),
            (copy_ref, 0, features, swapped_ref, x_ref.shape[0]),
        ],
        out_refs,
    )


def gather_last(place_ref, relay_ref, swapped_ref, *out_refs):
    features = swapped_ref.shape[1]
    gather_sequences(features, place_ref, [], [(relay_ref, 0, features, swapped_ref, 0)], out_refs)


def middle_part(place_ref, counts_ref, pieces_ref, *refs):
    three, last = refs[:6], refs[6:12]
    out_ref, wide, slim, probe, tangent, spread = refs[12:]
    copy, parity = place_ref[0], place_ref[2]
    length = three[3].shape[1]
    features = probe.shape[0]
    shards = pieces_ref.shape[0]
    inv_root = 1.0 / math.sqrt(HEAD)
    pair_lane, quad_lane = lane_of(PAIRS), lane_of(QUADS)
    top_row = lax.broadcasted_iota(jnp.int32, (8, LANES), 0) == 0
    wide_block = (2 * copy + parity + 1) // 2
    slim_block = 2 * copy

    def place(shard, start):
        first = start // BLOCKS
        shift = start - first * BLOCKS
        piece = pieces_ref[shard].astype(jnp.float32)
        pairs, quads = piece[:PAIRS], piece[PAIRS:]
        wide_values = [jnp.where(pair_lane < HALF, pairs, 0.0), jnp.where(pair_lane < HALF, 0.0, pairs)]
        slim_values = [jnp.where(quad_lane // QUARTER == at, quads, 0.0) for at in range(4)]
        for slab, block, values in ((wide, wide_block, wide_values), (slim, slim_block, slim_values)):
            values = jnp.concatenate(values, axis=0)
            before = slab[pl.ds(first, 8), :]
            slab[pl.ds(first, 8), :] = jnp.where(top_row & (block < shift), before, values[:8])
            slab[pl.ds(first + 8, USED - 8), :] = values[8:USED]
        return start + counts_ref[shard] // LANES

    lax.fori_loop(0, shards, place, jnp.int32(0), unroll=4)
    probe[:, :LANES] = wide[:features, :].astype(jnp.bfloat16)
    probe[:, LANES:] = slim[:features, :].astype(jnp.bfloat16)

    row = 0
    for tokens_ref, *_ in (three, last):
        count = tokens_ref.shape[0]
        product = jnp.dot(tokens_ref[...], probe[...], preferred_element_type=jnp.float32)
        wide_sum, slim_sum = product[:, :LANES], product[:, LANES:]
        wide_sum = wide_sum + turn(wide_sum, HALF)
        slim_sum = slim_sum + turn(slim_sum, HALF)
        slim_sum = slim_sum + turn(slim_sum, QUARTER)
        lane = lane_of(count)
        ordered = jnp.where(
            parity == 0,
            jnp.where(lane < HALF, wide_sum, slim_sum),
            jnp.where(lane < QUARTER, slim_sum, turn(wide_sum, QUARTER)),
        )
        tangent[row : row + count, :] = ordered[:, :HEAD].astype(jnp.bfloat16)
        row += count

    row = 0
    for _, _, key_ref, attn_ref, back_ref, centred_ref in (three, last):
        for at in range(key_ref.shape[0]):
            rows = slice(row, row + length)
            key_head, attn, back = key_ref[at], attn_ref[at], back_ref[at]
            score_tangent = inv_root * times_transposed(tangent[rows, :], key_head)
            mean_tangent = jnp.sum(attn * score_tangent, axis=1, keepdims=True)
            weight_tangent = attn * (score_tangent - mean_tangent)
            delta_tangent = jnp.sum(weight_tangent * back, axis=1, keepdims=True)
            grad_tangent = (weight_tangent * centred_ref[at] - attn * delta_tangent).astype(jnp.bfloat16)
            scaled = inv_root * jnp.dot(grad_tangent, key_head, preferred_element_type=jnp.float32)
            scaled = scaled.astype(jnp.bfloat16)

            def lay(wide_part, slim_part):
                for side in range(2):
                    spread[rows, side * HALF : (side + 1) * HALF] = wide_part
                for side in range(4):
                    spread[rows, LANES + side * QUARTER : LANES + (side + 1) * QUARTER] = slim_part

            @pl.when(parity == 0)
            def _():
                lay(scaled[:, :HALF], scaled[:, HALF:])

            @pl.when(parity == 1)
            def _():
                lay(scaled[:, QUARTER:], scaled[:, :QUARTER])

            row += length

    split = three[0].shape[0]
    term = jnp.dot(three[1][...], spread[:split, :], preferred_element_type=jnp.float32)
    term += jnp.dot(last[1][...], spread[split:, :], preferred_element_type=jnp.float32)
    wide[:features, :] = term[:, :LANES]
    slim[:features, :] = term[:, LANES:]

    def cut_out(shard, start):
        first = start // BLOCKS
        pairs = jnp.where(pair_lane < HALF, wide[pl.ds(first, PAIRS), :], wide[pl.ds(first + PAIRS, PAIRS), :])
        quads = by_quarter([slim[pl.ds(first + at * QUADS, QUADS), :] for at in range(4)])
        out_ref[shard] = jnp.concatenate([pairs, quads], axis=0).astype(jnp.bfloat16)
        return start + counts_ref[shard] // LANES

    lax.fori_loop(0, shards, cut_out, jnp.int32(0), unroll=4)


def add_groups(terms_ref, out_ref):
    for parity in range(2):

        def add(at, total):
            return total + terms_ref[at // ROW * 2 * ROW + lax.rem(at, ROW) + parity * ROW].astype(jnp.float32)

        out_ref[parity * WINDOW : (parity + 1) * WINDOW, :] = lax.fori_loop(
            0, terms_ref.shape[0] // 2, add, jnp.zeros((WINDOW, LANES), jnp.float32), unroll=4
        )


def update_shard(place_ref, counts_ref, sums_ref, probe_ref, hess_ref, out_ref, rows):
    shard = place_ref[1]
    shift = lax.rem(first_block(counts_ref, shard), BLOCKS)
    blocks = probe_ref.shape[0]

    def wide_part(head):
        pairs = sums_ref[head // 2, head % 2 * WINDOW : head % 2 * WINDOW + PAIRS, :]
        lane = WIDE[head][1]
        return jnp.concatenate([turn(pairs, lane - at * HALF) for at in range(2)], axis=0)

    def slim_part(head):
        quads = sums_ref[head // 2, head % 2 * WINDOW + PAIRS : (head % 2 + 1) * WINDOW, :]
        lane = SLIM[head][1]
        return jnp.concatenate([turn(quads, lane - at * QUARTER) for at in range(4)], axis=0)

    lane = lane_of(SPAN)
    rows[pl.ds(0, SPAN, stride=BLOCKS), :] = jnp.where(
        lane < HALF, wide_part(0), jnp.where(lane < 3 * QUARTER, slim_part(0), slim_part(1))
    )
    rows[pl.ds(1, SPAN, stride=BLOCKS), :] = jnp.where(lane < HALF, wide_part(1), wide_part(2))
    rows[pl.ds(2, SPAN, stride=BLOCKS), :] = jnp.where(
        lane < HALF, jnp.where(lane < QUARTER, slim_part(2), slim_part(3)), wide_part(3)
    )
    inner = lax.broadcasted_iota(jnp.int32, (blocks, LANES), 0)
    product = jnp.where(inner < counts_ref[shard] // LANES, rows[pl.ds(shift, blocks), :], 0.0)
    out_ref[...] = decay_rate * hess_ref[...] + (1.0 - decay_rate) * probe_ref[...].astype(jnp.float32) * product


def call(kernel, outs, operands, scalars, scratch=()):
    shapes = [jax.ShapeDtypeStruct(shape, dtype) for shape, dtype in outs]
    result = pl.pallas_call(
        kernel,
        out_shape=shapes,
        in_specs=[SMEM] * scalars + [VMEM] * (len(operands) - scalars),
        out_specs=[VMEM] * len(shapes),
        scratch_shapes=list(scratch),
        compiler_params=params(),
        name=kernel.__name__,
    )(*operands)
    return result if len(shapes) > 1 else result[0]


def body(tokens, queries, key_rows, value_rows, cotangent, probe_shards, hess_old, shard_counts):
    length, features = tokens.shape
    half = length // 2
    packed = 2 * HEADS * HEAD
    shards = shard_counts.shape[0]
    blocks = probe_shards.shape[1] // LANES
    bf16, f32 = jnp.bfloat16, jnp.float32
    slab = pltpu.VMEM((features + SPAN, LANES), f32)
    rows = pltpu.VMEM((BLOCKS * SPAN + 8, LANES), f32)
    at = lax.axis_index("dp")
    place = jnp.stack(
        [lax.axis_index("replica"), at, at // ROW % 2, lax.axis_index("tensor") % 2]
    ).astype(jnp.int32)

    def swap_copies(array):
        return lax.ppermute(array, "replica", [(0, 1), (1, 0)])

    def swap_cores(array):
        return lax.ppermute(array, "tensor", [(one, one ^ 1) for one in range(lax.axis_size("tensor"))])

    keep, to_x, to_copy = call(
        split_heads,
        [
            ((length, HEADS * HEAD), bf16),
            ((half, packed + features + packed), bf16),
            ((half, features + packed), bf16),
        ],
        (place, tokens, queries, key_rows, value_rows, cotangent),
        1,
    )
    from_x = lax.ppermute(to_x, "dp", [(one, one ^ ROW) for one in range(shards)])
    from_copy = swap_copies(to_copy)

    windows = call(
        pack_shard, [((shards, WINDOW, LANES), bf16)], (place, shard_counts, probe_shards), 2, (rows,)
    )
    pieces = lax.all_to_all(windows, "dp", 0, 0)

    relayed = swap_copies(from_x[:, packed:])
    swapped = swap_cores(
        jnp.concatenate([from_x[:, packed : packed + features], from_copy[:, :features]], axis=0)
    )
    swapped_last = swap_cores(relayed[:, :features])

    def gathered(count):
        square = ((count, length, length), f32)
        return [
            ((count * length, features), bf16),
            ((features, count * length), bf16),
            ((count, length, HEAD), bf16),
            square,
            square,
            square,
        ]

    three = call(gather_three, gathered(3), (place, tokens, keep, from_x, from_copy, swapped), 1)
    last = call(gather_last, gathered(1), (place, relayed, swapped_last), 1)

    term_windows = call(
        middle_part,
        [((shards, WINDOW, LANES), bf16)],
        (place, shard_counts, pieces, *three, *last),
        2,
        (
            slab,
            slab,
            pltpu.VMEM((features, 2 * LANES), bf16),
            pltpu.VMEM((4 * length, HEAD), bf16),
            pltpu.VMEM((4 * length, 2 * LANES), bf16),
        ),
    )
    terms = lax.all_to_all(term_windows, "dp", 0, 0)
    summed = call(add_groups, [((2 * WINDOW, LANES), f32)], (terms,), 0)
    sums = lax.all_gather(summed, "replica", axis=0)
    updated = call(
        update_shard,
        [((blocks, LANES), f32)],
        (place, shard_counts, sums, probe_shards.reshape(blocks, LANES), hess_old.reshape(blocks, LANES)),
        2,
        (rows,),
    )
    return updated.reshape(1, blocks * LANES)


def solution(mesh):
    placed = (
        P(("dp", "replica"), None),
        P(("dp", "replica"), "tensor"),
        P(("dp", "replica"), "tensor"),
        P(("dp", "replica"), "tensor"),
        P(("dp", "replica"), "tensor"),
        P("tensor", "dp"),
        P("tensor", "dp"),
        P(),
    )
    return jax.shard_map(
        body, mesh=mesh, in_specs=placed, out_specs=P("tensor", "dp"), check_vma=False
    )
```

```python
import math

import jax
import jax.numpy as jnp
from jax import lax
from jax.experimental import pallas as pl
from jax.experimental.pallas import tpu as pltpu
from jax.sharding import PartitionSpec as P

HEAD = 96
LANES = 128
decay_rate = 0.99

ROW = 8

HEADS = 4

BLOCKS = 3
WIDE = ((0, 0), (1, 0), (1, 64), (2, 64))
SLIM = ((0, 64), (0, 96), (2, 0), (2, 32))
SPAN = 64
PAIRS = SPAN // 2
QUADS = SPAN // 4
WINDOW = PAIRS + QUADS
USED = 56
HALF = LANES // 2
QUARTER = LANES // 4

VMEM = pl.BlockSpec(memory_space=pltpu.VMEM)
SMEM = pl.BlockSpec(memory_space=pltpu.SMEM)
HBM = pl.BlockSpec(memory_space=pltpu.HBM)


def lane_of(rows):
    return lax.broadcasted_iota(jnp.int32, (rows, LANES), 1)


def turn(values, lanes):
    lanes = lanes % LANES
    return values if lanes == 0 else pltpu.roll(values, lanes, 1)


def first_block(counts_ref, shard):
    return lax.fori_loop(0, shard, lambda at, total: total + counts_ref[at] // LANES, jnp.int32(0))


def by_quarter(parts):
    lane = lane_of(parts[0].shape[0])
    low = jnp.where(lane < QUARTER, parts[0], parts[1])
    high = jnp.where(lane < 3 * QUARTER, parts[2], parts[3])
    return jnp.where(lane < HALF, low, high)


def pack_shard(place_ref, counts_hbm, probe_hbm, out_ref, rows, counts_ref, probe_ref, sems):
    copy = place_ref[0]
    loads = [
        pltpu.make_async_copy(counts_hbm, counts_ref, sems.at[0]),
        pltpu.make_async_copy(probe_hbm, probe_ref, sems.at[1]),
    ]
    for load in loads:
        load.start()
    rows[...] = jnp.zeros_like(rows)
    for load in loads:
        load.wait()
    shift = lax.rem(first_block(counts_ref, place_ref[1]), BLOCKS)
    for block in range(probe_ref.shape[1] // LANES):
        rows[pl.ds(shift + block, 1), :] = probe_ref[0:1, block * LANES : (block + 1) * LANES].astype(jnp.float32)

    def window(head):
        block, lane = WIDE[head]
        wide = rows[pl.ds(block, SPAN, stride=BLOCKS), :]
        pairs = jnp.where(lane_of(PAIRS) < HALF, turn(wide[:PAIRS], -lane), turn(wide[PAIRS:], HALF - lane))
        block, lane = SLIM[head]
        slim = rows[pl.ds(block, SPAN, stride=BLOCKS), :]
        quads = by_quarter(
            [turn(slim[at * QUADS : (at + 1) * QUADS], at * QUARTER - lane) for at in range(4)]
        )
        return jnp.concatenate([pairs, quads], axis=0).astype(jnp.bfloat16)

    for which in range(2):

        @pl.when(copy == which)
        def _():
            even, odd = window(2 * which), window(2 * which + 1)

            def store(at, carry):
                first = at // ROW * 2 * ROW + lax.rem(at, ROW)
                out_ref[first] = even
                out_ref[first + ROW] = odd
                return carry

            lax.fori_loop(0, out_ref.shape[0] // 2, store, 0, unroll=4)


def split_heads(
    place_ref, tokens_hbm, query_hbm, key_hbm, value_hbm, cot_hbm, keep_ref, x_ref, copy_ref, held, sems
):
    copy, parity, core = place_ref[0], place_ref[2], place_ref[3]
    length, features = tokens_hbm.shape
    half = length // 2
    packed = 2 * HEADS * HEAD
    arrays = [held.at[at] for at in range(HEADS)]
    loads = [
        pltpu.make_async_copy(source, target, sems.at[at])
        for at, (source, target) in enumerate(zip((query_hbm, key_hbm, value_hbm, cot_hbm), arrays))
    ]
    tokens = tokens_hbm.at[pl.ds(pl.multiple_of(core * half, half), half), :]
    loads.append(pltpu.make_async_copy(tokens, x_ref.at[:, pl.ds(packed, features)], sems.at[4]))
    loads.append(pltpu.make_async_copy(tokens, copy_ref.at[:, pl.ds(0, features)], sems.at[5]))
    for load in loads:
        load.start()
    for load in loads[:HEADS]:
        load.wait()

    def put(head, target_ref, start):
        for side in range(2):
            for at, ref in enumerate(arrays):
                to = start + (side * HEADS + at) * HEAD
                target_ref[:, to : to + HEAD] = ref[side * half : (side + 1) * half, head * HEAD : (head + 1) * HEAD]

    for mine in range(HEADS):

        @pl.when(2 * copy + parity == mine)
        def _():
            for at, ref in enumerate(arrays):
                keep_ref[:, at * HEAD : (at + 1) * HEAD] = ref[:, mine * HEAD : (mine + 1) * HEAD]
            put(mine ^ 1, x_ref, 0)
            put(mine ^ 3, x_ref, packed + features)
            put(mine ^ 2, copy_ref, features)

    for load in loads[HEADS:]:
        load.wait()


def attention_part(heads):
    length = heads.shape[0]
    query, key_head, value_head, cot_head = (heads[:, at * HEAD : (at + 1) * HEAD] for at in range(HEADS))
    inv_root = 1.0 / math.sqrt(HEAD)
    causal = lax.broadcasted_iota(jnp.int32, (length, length), 0) >= lax.broadcasted_iota(
        jnp.int32, (length, length), 1
    )
    scores = inv_root * times_transposed(query, key_head)
    scores = jnp.where(causal, scores, jnp.float32(-1e30))
    expo_terms = jnp.exp(scores - jnp.max(scores, axis=1, keepdims=True))
    attn = expo_terms / jnp.sum(expo_terms, axis=1, keepdims=True)
    back = times_transposed(cot_head, value_head)
    padded_key = jnp.concatenate([key_head, jnp.zeros((length, LANES - HEAD), key_head.dtype)], axis=1)
    return padded_key, attn, back, back - jnp.sum(attn * back, axis=1, keepdims=True)


def times_transposed(left, right):
    return lax.dot_general(left, right, (((1,), (1,)), ((), ())), preferred_element_type=jnp.float32)


def join_halves(core, mine_ref, mine_at, heads_at, other_ref, other_row, tokens_ref, row):
    half, features = mine_ref.shape[0], tokens_ref.shape[1]
    side = HEADS * HEAD
    tokens_ref[pl.ds(pl.multiple_of(row + core * half, half), half), :] = mine_ref[:, mine_at : mine_at + features]
    tokens_ref[pl.ds(pl.multiple_of(row + (1 - core) * half, half), half), :] = other_ref[
        other_row : other_row + half, :
    ]
    return jnp.concatenate(
        [mine_ref[:, heads_at : heads_at + side], mine_ref[:, heads_at + side : heads_at + 2 * side]], axis=0
    )


def prepare(
    place_ref,
    tokens_hbm,
    probe_hbm,
    hess_hbm,
    keep_ref,
    x_ref,
    copy_ref,
    swapped_ref,
    tokens_out,
    turned_out,
    key_ref,
    attn_ref,
    back_ref,
    centred_ref,
    factor_ref,
    base_ref,
    tokens_ref,
    turned_ref,
    probe_ref,
    hess_ref,
    sems,
):
    core = place_ref[3]
    length, features = tokens_hbm.shape
    packed = 2 * HEADS * HEAD
    loads = [
        pltpu.make_async_copy(tokens_hbm, tokens_ref.at[pl.ds(0, length), :], sems.at[0]),
        pltpu.make_async_copy(probe_hbm, probe_ref, sems.at[1]),
        pltpu.make_async_copy(hess_hbm, hess_ref, sems.at[2]),
    ]
    for load in loads:
        load.start()
    heads_of = [
        keep_ref[...],
        join_halves(core, x_ref, packed, 0, swapped_ref, 0, tokens_ref, length),
        join_halves(core, copy_ref, 0, features, swapped_ref, x_ref.shape[0], tokens_ref, 2 * length),
    ]
    loads[0].wait()
    stores = [
        pltpu.make_async_copy(tokens_ref, tokens_out, sems.at[3]),
        pltpu.make_async_copy(turned_ref, turned_out, sems.at[4]),
    ]
    stores[0].start()
    turned_ref[...] = tokens_ref[...].T
    stores[1].start()
    for at, heads in enumerate(heads_of):
        key_ref[at], attn_ref[at], back_ref[at], centred_ref[at] = attention_part(heads)
    for load in loads[1:]:
        load.wait()
    for block in range(probe_ref.shape[1] // LANES):
        lanes = slice(block * LANES, (block + 1) * LANES)
        factor_ref[block : block + 1, :] = (1.0 - decay_rate) * probe_ref[0:1, lanes].astype(jnp.float32)
        base_ref[block : block + 1, :] = decay_rate * hess_ref[0:1, lanes]
    for store in stores:
        store.wait()


def middle_part(
    place_ref,
    counts_ref,
    tokens_hbm,
    turned_hbm,
    pieces_ref,
    relay_ref,
    swapped_ref,
    key_ref,
    attn_ref,
    back_ref,
    centred_ref,
    out_ref,
    wide,
    slim,
    probe,
    tangent,
    spread,
    tokens,
    turned,
    last_tokens,
    last_turned,
    sems,
):
    loads = [
        pltpu.make_async_copy(tokens_hbm, tokens, sems.at[0]),
        pltpu.make_async_copy(turned_hbm, turned, sems.at[1]),
    ]
    for load in loads:
        load.start()
    copy, parity, core = place_ref[0], place_ref[2], place_ref[3]
    length = attn_ref.shape[1]
    features = probe.shape[0]
    shards = pieces_ref.shape[0]
    inv_root = 1.0 / math.sqrt(HEAD)
    pair_lane, quad_lane = lane_of(PAIRS), lane_of(QUADS)
    top_row = lax.broadcasted_iota(jnp.int32, (8, LANES), 0) == 0
    wide_block = (2 * copy + parity + 1) // 2
    slim_block = 2 * copy

    def place(shard, start):
        first = start // BLOCKS
        shift = start - first * BLOCKS
        piece = pieces_ref[shard].astype(jnp.float32)
        pairs, quads = piece[:PAIRS], piece[PAIRS:]
        wide_values = [jnp.where(pair_lane < HALF, pairs, 0.0), jnp.where(pair_lane < HALF, 0.0, pairs)]
        slim_values = [jnp.where(quad_lane // QUARTER == at, quads, 0.0) for at in range(4)]
        for slab, block, values in ((wide, wide_block, wide_values), (slim, slim_block, slim_values)):
            values = jnp.concatenate(values, axis=0)
            ours = jnp.logical_not(top_row & (block < shift))
            pltpu.store(slab.at[pl.ds(first, 8), :], values[:8], mask=ours)
            slab[pl.ds(first + 8, USED - 8), :] = values[8:USED]
        return start + counts_ref[shard] // LANES

    last_heads = join_halves(core, relay_ref, 0, features, swapped_ref, 0, last_tokens, 0)
    last_turned[...] = last_tokens[...].T
    parts = [(key_ref[at], attn_ref[at], back_ref[at], centred_ref[at]) for at in range(key_ref.shape[0])]
    parts.append(attention_part(last_heads))
    lax.fori_loop(0, shards, place, jnp.int32(0), unroll=4)
    for load in loads:
        load.wait()
    probe[:, :LANES] = wide[:features, :].astype(jnp.bfloat16)
    probe[:, LANES:] = slim[:features, :].astype(jnp.bfloat16)

    row = 0
    for tokens_ref in (tokens, last_tokens):
        count = tokens_ref.shape[0]
        product = jnp.dot(tokens_ref[...], probe[...], preferred_element_type=jnp.float32)
        wide_sum, slim_sum = product[:, :LANES], product[:, LANES:]
        wide_sum = wide_sum + turn(wide_sum, HALF)
        slim_sum = slim_sum + turn(slim_sum, HALF)
        slim_sum = slim_sum + turn(slim_sum, QUARTER)
        lane = lane_of(count)
        ordered = jnp.where(
            parity == 0,
            jnp.where(lane < HALF, wide_sum, slim_sum),
            jnp.where(lane < QUARTER, slim_sum, turn(wide_sum, QUARTER)),
        )
        tangent[row : row + count, :] = ordered.astype(jnp.bfloat16)
        row += count

    for at, (key_head, attn, back, centred) in enumerate(parts):
        rows = slice(at * length, (at + 1) * length)
        score_tangent = inv_root * times_transposed(tangent[rows, :], key_head)
        mean_tangent = jnp.sum(attn * score_tangent, axis=1, keepdims=True)
        weight_tangent = attn * (score_tangent - mean_tangent)
        delta_tangent = jnp.sum(weight_tangent * back, axis=1, keepdims=True)
        grad_tangent = (weight_tangent * centred - attn * delta_tangent).astype(jnp.bfloat16)
        scaled = inv_root * jnp.dot(grad_tangent, key_head, preferred_element_type=jnp.float32)
        turns = [turn(scaled, at * QUARTER) for at in range(4)]
        wide_part = jnp.where(
            parity == 0,
            jnp.where(lane_of(length) < HALF, scaled, turns[2]),
            jnp.where(lane_of(length) < HALF, turns[3], turns[1]),
        )
        slim_part = jnp.where(
            parity == 0, by_quarter([turns[2], turns[3], scaled, turns[1]]), by_quarter(turns)
        )
        spread[rows, :LANES] = wide_part.astype(jnp.bfloat16)
        spread[rows, LANES:] = slim_part.astype(jnp.bfloat16)

    split = tokens.shape[0]
    term = jnp.dot(turned[...], spread[:split, :], preferred_element_type=jnp.float32)
    term += jnp.dot(last_turned[...], spread[split:, :], preferred_element_type=jnp.float32)
    wide[:features, :] = term[:, :LANES]
    slim[:features, :] = term[:, LANES:]

    def cut_out(shard, start):
        first = start // BLOCKS
        pairs = jnp.where(pair_lane < HALF, wide[pl.ds(first, PAIRS), :], wide[pl.ds(first + PAIRS, PAIRS), :])
        quads = by_quarter([slim[pl.ds(first + at * QUADS, QUADS), :] for at in range(4)])
        out_ref[shard] = jnp.concatenate([pairs, quads], axis=0).astype(jnp.bfloat16)
        return start + counts_ref[shard] // LANES

    lax.fori_loop(0, shards, cut_out, jnp.int32(0), unroll=4)


def add_groups(terms_ref, out_ref):
    for parity in range(2):

        def add(at, total):
            return total + terms_ref[at // ROW * 2 * ROW + lax.rem(at, ROW) + parity * ROW].astype(jnp.float32)

        out_ref[parity * WINDOW : (parity + 1) * WINDOW, :] = lax.fori_loop(
            0, terms_ref.shape[0] // 2, add, jnp.zeros((WINDOW, LANES), jnp.float32), unroll=4
        )


def update_shard(place_ref, counts_ref, sums_ref, factor_ref, base_ref, out_ref, rows):
    shard = place_ref[1]
    shift = lax.rem(first_block(counts_ref, shard), BLOCKS)
    blocks = factor_ref.shape[0]

    def wide_part(head):
        pairs = sums_ref[head // 2, head % 2 * WINDOW : head % 2 * WINDOW + PAIRS, :]
        lane = WIDE[head][1]
        return jnp.concatenate([turn(pairs, lane - at * HALF) for at in range(2)], axis=0)

    def slim_part(head):
        quads = sums_ref[head // 2, head % 2 * WINDOW + PAIRS : (head % 2 + 1) * WINDOW, :]
        lane = SLIM[head][1]
        return jnp.concatenate([turn(quads, lane - at * QUARTER) for at in range(4)], axis=0)

    lane = lane_of(SPAN)
    rows[pl.ds(0, SPAN, stride=BLOCKS), :] = jnp.where(
        lane < HALF, wide_part(0), jnp.where(lane < 3 * QUARTER, slim_part(0), slim_part(1))
    )
    rows[pl.ds(1, SPAN, stride=BLOCKS), :] = jnp.where(lane < HALF, wide_part(1), wide_part(2))
    rows[pl.ds(2, SPAN, stride=BLOCKS), :] = jnp.where(
        lane < HALF, jnp.where(lane < QUARTER, slim_part(2), slim_part(3)), wide_part(3)
    )
    inner = lax.broadcasted_iota(jnp.int32, (blocks, LANES), 0)
    product = jnp.where(inner < counts_ref[shard] // LANES, rows[pl.ds(shift, blocks), :], 0.0)
    updated = base_ref[...] + factor_ref[...] * product
    for block in range(blocks):
        out_ref[0:1, block * LANES : (block + 1) * LANES] = updated[block : block + 1, :]


def call(kernel, outs, specs, operands, mebibytes, scratch=(), in_hbm=0):
    shapes = [
        (pltpu.HBM if at < in_hbm else jax.ShapeDtypeStruct)(shape, dtype) for at, (shape, dtype) in enumerate(outs)
    ]
    specs = specs + [VMEM] * (len(operands) - len(specs))
    operands = [
        pltpu.with_memory_space_constraint(operand, pltpu.HBM) if spec is HBM else operand
        for spec, operand in zip(specs, operands)
    ]
    result = pl.pallas_call(
        kernel,
        out_shape=shapes,
        in_specs=specs,
        out_specs=[HBM] * in_hbm + [VMEM] * (len(shapes) - in_hbm),
        scratch_shapes=list(scratch),
        compiler_params=pltpu.CompilerParams(vmem_limit_bytes=mebibytes * 1024 * 1024),
        name=kernel.__name__,
    )(*operands)
    return result if len(shapes) > 1 else result[0]


def body(tokens, queries, key_rows, value_rows, cotangent, probe_shards, hess_old, shard_counts):
    length, features = tokens.shape
    half = length // 2
    packed = 2 * HEADS * HEAD
    shards = shard_counts.shape[0]
    blocks = probe_shards.shape[1] // LANES
    bf16, f32 = jnp.bfloat16, jnp.float32
    slab = pltpu.VMEM((features + SPAN, LANES), f32)
    rows = pltpu.VMEM((BLOCKS * SPAN + 8, LANES), f32)
    at = lax.axis_index("dp")
    place = jnp.stack(
        [lax.axis_index("replica"), at, at // ROW % 2, lax.axis_index("tensor") % 2]
    ).astype(jnp.int32)

    def swap_copies(array):
        return lax.ppermute(array, "replica", [(0, 1), (1, 0)])

    def swap_cores(array):
        return lax.ppermute(array, "tensor", [(one, one ^ 1) for one in range(lax.axis_size("tensor"))])

    keep, to_x, to_copy = call(
        split_heads,
        [
            ((length, HEADS * HEAD), bf16),
            ((half, packed + features + packed), bf16),
            ((half, features + packed), bf16),
        ],
        [SMEM] + [HBM] * 5,
        (place, tokens, queries, key_rows, value_rows, cotangent),
        8,
        (pltpu.VMEM((HEADS, *queries.shape), bf16), pltpu.SemaphoreType.DMA((6,))),
    )
    from_x = lax.ppermute(to_x, "dp", [(one, one ^ ROW) for one in range(shards)])
    from_copy = swap_copies(to_copy)

    windows = call(
        pack_shard,
        [((shards, WINDOW, LANES), bf16)],
        [SMEM, HBM, HBM],
        (place, shard_counts, probe_shards),
        8,
        (
            rows,
            pltpu.SMEM(shard_counts.shape, jnp.int32),
            pltpu.VMEM(probe_shards.shape, bf16),
            pltpu.SemaphoreType.DMA((2,)),
        ),
    )
    pieces = lax.all_to_all(windows, "dp", 0, 0)

    relayed = swap_copies(from_x[:, packed:])
    swapped = swap_cores(
        jnp.concatenate([from_x[:, packed : packed + features], from_copy[:, :features]], axis=0)
    )
    swapped_last = swap_cores(relayed[:, :features])

    square = ((3, length, length), f32)
    update_part = ((blocks, LANES), f32)
    three_tokens = pltpu.VMEM((3 * length, features), bf16)
    three_turned = pltpu.VMEM((features, 3 * length), bf16)
    all_tokens, all_turned, *parts, factor, base = call(
        prepare,
        [
            ((3 * length, features), bf16),
            ((features, 3 * length), bf16),
            ((3, length, LANES), bf16),
            square,
            square,
            square,
            update_part,
            update_part,
        ],
        [SMEM, HBM, HBM, HBM],
        (place, tokens, probe_shards, hess_old, keep, from_x, from_copy, swapped),
        16,
        (
            three_tokens,
            three_turned,
            pltpu.VMEM(probe_shards.shape, bf16),
            pltpu.VMEM(hess_old.shape, f32),
            pltpu.SemaphoreType.DMA((5,)),
        ),
        in_hbm=2,
    )
    term_windows = call(
        middle_part,
        [((shards, WINDOW, LANES), bf16)],
        [SMEM, SMEM, HBM, HBM],
        (place, shard_counts, all_tokens, all_turned, pieces, relayed, swapped_last, *parts),
        24,
        (
            slab,
            slab,
            pltpu.VMEM((features, 2 * LANES), bf16),
            pltpu.VMEM((4 * length, LANES), bf16),
            pltpu.VMEM((4 * length, 2 * LANES), bf16),
            three_tokens,
            three_turned,
            pltpu.VMEM((length, features), bf16),
            pltpu.VMEM((features, length), bf16),
            pltpu.SemaphoreType.DMA((2,)),
        ),
    )
    terms = lax.all_to_all(term_windows, "dp", 0, 0)
    summed = call(add_groups, [((2 * WINDOW, LANES), f32)], [], (terms,), 8)
    sums = lax.all_gather(summed, "replica", axis=0)
    return call(
        update_shard,
        [((1, blocks * LANES), f32)],
        [SMEM, SMEM],
        (place, shard_counts, sums, factor, base),
        8,
        (rows,),
    )


def solution(mesh):
    placed = (
        P(("dp", "replica"), None),
        P(("dp", "replica"), "tensor"),
        P(("dp", "replica"), "tensor"),
        P(("dp", "replica"), "tensor"),
        P(("dp", "replica"), "tensor"),
        P("tensor", "dp"),
        P("tensor", "dp"),
        P(),
    )
    return jax.shard_map(
        body, mesh=mesh, in_specs=placed, out_specs=P("tensor", "dp"), check_vma=False
    )
```

```python
import math

import jax
import jax.numpy as jnp
from jax import lax
from jax.experimental import pallas as pl
from jax.experimental.pallas import tpu as pltpu
from jax.sharding import PartitionSpec as P

HEAD = 96
LANES = 128
decay_rate = 0.99

ROW = 8

HEADS = 4

BLOCKS = 3
WIDE = ((0, 0), (1, 0), (1, 64), (2, 64))
SLIM = ((0, 64), (0, 96), (2, 0), (2, 32))
SPAN = 64
PAIRS = SPAN // 2
QUADS = SPAN // 4
WINDOW = PAIRS + QUADS
USED = 56
HALF = LANES // 2
QUARTER = LANES // 4

VMEM = pl.BlockSpec(memory_space=pltpu.VMEM)
SMEM = pl.BlockSpec(memory_space=pltpu.SMEM)
HBM = pl.BlockSpec(memory_space=pltpu.HBM)


def lane_of(rows):
    return lax.broadcasted_iota(jnp.int32, (rows, LANES), 1)


def turn(values, lanes):
    lanes = lanes % LANES
    return values if lanes == 0 else pltpu.roll(values, lanes, 1)


def first_block(counts_ref, shard):
    return lax.fori_loop(0, shard, lambda at, total: total + counts_ref[at] // LANES, jnp.int32(0))


def by_quarter(parts):
    lane = lane_of(parts[0].shape[0])
    low = jnp.where(lane < QUARTER, parts[0], parts[1])
    high = jnp.where(lane < 3 * QUARTER, parts[2], parts[3])
    return jnp.where(lane < HALF, low, high)


def pack(
    place_ref,
    counts_hbm,
    probe_hbm,
    tokens_hbm,
    query_hbm,
    key_hbm,
    value_hbm,
    cot_hbm,
    windows_hbm,
    keep_ref,
    x_ref,
    copy_ref,
    rows,
    counts_ref,
    probe_ref,
    windows,
    held,
    sems,
):
    copy, parity, core = place_ref[0], place_ref[2], place_ref[3]
    length, features = tokens_hbm.shape
    half = length // 2
    packed = 2 * HEADS * HEAD
    shard_loads = [
        pltpu.make_async_copy(counts_hbm, counts_ref, sems.at[0]),
        pltpu.make_async_copy(probe_hbm, probe_ref, sems.at[1]),
    ]
    arrays = [held.at[at] for at in range(HEADS)]
    head_loads = [
        pltpu.make_async_copy(source, target, sems.at[2 + at])
        for at, (source, target) in enumerate(zip((query_hbm, key_hbm, value_hbm, cot_hbm), arrays))
    ]
    tokens = tokens_hbm.at[pl.ds(pl.multiple_of(core * half, half), half), :]
    token_loads = [
        pltpu.make_async_copy(tokens, x_ref.at[:, pl.ds(packed, features)], sems.at[6]),
        pltpu.make_async_copy(tokens, copy_ref.at[:, pl.ds(0, features)], sems.at[7]),
    ]
    for load in shard_loads + head_loads + token_loads:
        load.start()
    rows[...] = jnp.zeros_like(rows)
    for load in shard_loads:
        load.wait()

    shift = lax.rem(first_block(counts_ref, place_ref[1]), BLOCKS)
    for block in range(probe_ref.shape[1] // LANES):
        rows[pl.ds(shift + block, 1), :] = probe_ref[0:1, block * LANES : (block + 1) * LANES].astype(jnp.float32)

    def window(head):
        block, lane = WIDE[head]
        wide = rows[pl.ds(block, SPAN, stride=BLOCKS), :]
        pairs = jnp.where(lane_of(PAIRS) < HALF, turn(wide[:PAIRS], -lane), turn(wide[PAIRS:], HALF - lane))
        block, lane = SLIM[head]
        slim = rows[pl.ds(block, SPAN, stride=BLOCKS), :]
        quads = by_quarter(
            [turn(slim[at * QUADS : (at + 1) * QUADS], at * QUARTER - lane) for at in range(4)]
        )
        return jnp.concatenate([pairs, quads], axis=0).astype(jnp.bfloat16)

    for which in range(2):

        @pl.when(copy == which)
        def _():
            even, odd = window(2 * which), window(2 * which + 1)

            def store(at, carry):
                first = at // ROW * 2 * ROW + lax.rem(at, ROW)
                windows[first] = even
                windows[first + ROW] = odd
                return carry

            lax.fori_loop(0, windows.shape[0] // 2, store, 0, unroll=4)

    leave = pltpu.make_async_copy(windows, windows_hbm, sems.at[8])
    leave.start()
    for load in head_loads:
        load.wait()

    def put(head, target_ref, start):
        for side in range(2):
            for at, ref in enumerate(arrays):
                to = start + (side * HEADS + at) * HEAD
                target_ref[:, to : to + HEAD] = ref[side * half : (side + 1) * half, head * HEAD : (head + 1) * HEAD]

    for mine in range(HEADS):

        @pl.when(2 * copy + parity == mine)
        def _():
            for at, ref in enumerate(arrays):
                keep_ref[:, at * HEAD : (at + 1) * HEAD] = ref[:, mine * HEAD : (mine + 1) * HEAD]
            put(mine ^ 1, x_ref, 0)
            put(mine ^ 3, x_ref, packed + features)
            put(mine ^ 2, copy_ref, features)

    for load in token_loads:
        load.wait()
    leave.wait()


def attention_part(heads):
    length = heads.shape[0]
    query, key_head, value_head, cot_head = (heads[:, at * HEAD : (at + 1) * HEAD] for at in range(HEADS))
    inv_root = 1.0 / math.sqrt(HEAD)
    causal = lax.broadcasted_iota(jnp.int32, (length, length), 0) >= lax.broadcasted_iota(
        jnp.int32, (length, length), 1
    )
    scores = inv_root * times_transposed(query, key_head)
    scores = jnp.where(causal, scores, jnp.float32(-1e30))
    expo_terms = jnp.exp(scores - jnp.max(scores, axis=1, keepdims=True))
    attn = expo_terms / jnp.sum(expo_terms, axis=1, keepdims=True)
    back = times_transposed(cot_head, value_head)
    padded_key = jnp.concatenate([key_head, jnp.zeros((length, LANES - HEAD), key_head.dtype)], axis=1)
    return padded_key, attn, back, back - jnp.sum(attn * back, axis=1, keepdims=True)


def times_transposed(left, right):
    return lax.dot_general(left, right, (((1,), (1,)), ((), ())), preferred_element_type=jnp.float32)


def join_halves(core, mine_ref, mine_at, heads_at, other_ref, other_row, tokens_ref, row):
    half, features = mine_ref.shape[0], tokens_ref.shape[1]
    side = HEADS * HEAD
    tokens_ref[pl.ds(pl.multiple_of(row + core * half, half), half), :] = mine_ref[:, mine_at : mine_at + features]
    tokens_ref[pl.ds(pl.multiple_of(row + (1 - core) * half, half), half), :] = other_ref[
        other_row : other_row + half, :
    ]
    return jnp.concatenate(
        [mine_ref[:, heads_at : heads_at + side], mine_ref[:, heads_at + side : heads_at + 2 * side]], axis=0
    )


def prepare(
    place_ref,
    tokens_hbm,
    probe_hbm,
    hess_hbm,
    keep_ref,
    x_ref,
    copy_ref,
    swapped_ref,
    tokens_out,
    turned_out,
    key_ref,
    attn_ref,
    back_ref,
    centred_ref,
    factor_ref,
    base_ref,
    tokens_ref,
    turned_ref,
    probe_ref,
    hess_ref,
    sems,
):
    core = place_ref[3]
    length, features = tokens_hbm.shape
    packed = 2 * HEADS * HEAD
    loads = [
        pltpu.make_async_copy(tokens_hbm, tokens_ref.at[pl.ds(0, length), :], sems.at[0]),
        pltpu.make_async_copy(probe_hbm, probe_ref, sems.at[1]),
        pltpu.make_async_copy(hess_hbm, hess_ref, sems.at[2]),
    ]
    for load in loads:
        load.start()
    heads_of = [
        keep_ref[...],
        join_halves(core, x_ref, packed, 0, swapped_ref, 0, tokens_ref, length),
        join_halves(core, copy_ref, 0, features, swapped_ref, x_ref.shape[0], tokens_ref, 2 * length),
    ]
    loads[0].wait()
    stores = [
        pltpu.make_async_copy(tokens_ref, tokens_out, sems.at[3]),
        pltpu.make_async_copy(turned_ref, turned_out, sems.at[4]),
    ]
    stores[0].start()
    turned_ref[...] = tokens_ref[...].T
    stores[1].start()
    for at, heads in enumerate(heads_of):
        key_ref[at], attn_ref[at], back_ref[at], centred_ref[at] = attention_part(heads)
    for load in loads[1:]:
        load.wait()
    for block in range(probe_ref.shape[1] // LANES):
        lanes = slice(block * LANES, (block + 1) * LANES)
        factor_ref[block : block + 1, :] = (1.0 - decay_rate) * probe_ref[0:1, lanes].astype(jnp.float32)
        base_ref[block : block + 1, :] = decay_rate * hess_ref[0:1, lanes]
    for store in stores:
        store.wait()


def middle_part(
    place_ref,
    counts_ref,
    tokens_hbm,
    turned_hbm,
    pieces_ref,
    relay_ref,
    swapped_ref,
    key_ref,
    attn_ref,
    back_ref,
    centred_ref,
    out_ref,
    wide,
    slim,
    probe,
    spread,
    tokens,
    turned,
    sems,
):
    last = tokens_hbm.shape[0]
    load_tokens = pltpu.make_async_copy(tokens_hbm, tokens.at[pl.ds(0, last), :], sems.at[0])
    load_turned = pltpu.make_async_copy(turned_hbm, turned.at[:, pl.ds(0, last)], sems.at[1])
    load_tokens.start()
    copy, parity, core = place_ref[0], place_ref[2], place_ref[3]
    length = attn_ref.shape[1]
    features = probe.shape[0]
    shards = pieces_ref.shape[0]
    inv_root = 1.0 / math.sqrt(HEAD)
    pair_lane, quad_lane = lane_of(PAIRS), lane_of(QUADS)
    top_row = lax.broadcasted_iota(jnp.int32, (8, LANES), 0) == 0
    wide_block = (2 * copy + parity + 1) // 2
    slim_block = 2 * copy

    def place(shard, start):
        first = start // BLOCKS
        shift = start - first * BLOCKS
        piece = pieces_ref[shard].astype(jnp.float32)
        pairs, quads = piece[:PAIRS], piece[PAIRS:]
        wide_values = [jnp.where(pair_lane < HALF, pairs, 0.0), jnp.where(pair_lane < HALF, 0.0, pairs)]
        slim_values = [jnp.where(quad_lane // QUARTER == at, quads, 0.0) for at in range(4)]
        for slab, block, values in ((wide, wide_block, wide_values), (slim, slim_block, slim_values)):
            values = jnp.concatenate(values, axis=0)
            ours = jnp.logical_not(top_row & (block < shift))
            pltpu.store(slab.at[pl.ds(first, 8), :], values[:8], mask=ours)
            slab[pl.ds(first + 8, USED - 8), :] = values[8:USED]
        return start + counts_ref[shard] // LANES

    last_heads = join_halves(core, relay_ref, 0, features, swapped_ref, 0, tokens, last)
    turned[:, last:] = tokens[last:, :].T
    parts = [(key_ref[at], attn_ref[at], back_ref[at], centred_ref[at]) for at in range(key_ref.shape[0])]
    parts.append(attention_part(last_heads))
    lax.fori_loop(0, shards, place, jnp.int32(0), unroll=16)
    load_tokens.wait()
    load_turned.start()
    probe[:, :LANES] = wide[:features, :].astype(jnp.bfloat16)
    probe[:, LANES:] = slim[:features, :].astype(jnp.bfloat16)

    product = jnp.dot(tokens[...], probe[...], preferred_element_type=jnp.float32)
    wide_sum, slim_sum = product[:, :LANES], product[:, LANES:]
    wide_sum = wide_sum + turn(wide_sum, HALF)
    slim_sum = slim_sum + turn(slim_sum, HALF)
    slim_sum = slim_sum + turn(slim_sum, QUARTER)
    lane = lane_of(product.shape[0])
    tangent = jnp.where(
        parity == 0,
        jnp.where(lane < HALF, wide_sum, slim_sum),
        jnp.where(lane < QUARTER, slim_sum, turn(wide_sum, QUARTER)),
    ).astype(jnp.bfloat16)

    keys, attns, backs, centreds = zip(*parts)
    cuts = [slice(at * length, (at + 1) * length) for at in range(len(parts))]
    score_tangents = [inv_root * times_transposed(tangent[cut], key_head) for cut, key_head in zip(cuts, keys)]
    means = [jnp.sum(attn * score, axis=1, keepdims=True) for attn, score in zip(attns, score_tangents)]
    weights = [attn * (score - mean) for attn, score, mean in zip(attns, score_tangents, means)]
    deltas = [jnp.sum(weight * back, axis=1, keepdims=True) for weight, back in zip(weights, backs)]
    grads = [
        (weight * centred - attn * delta).astype(jnp.bfloat16)
        for weight, centred, attn, delta in zip(weights, centreds, attns, deltas)
    ]
    lane = lane_of(length)
    for cut, grad, key_head in zip(cuts, grads, keys):
        scaled = inv_root * jnp.dot(grad, key_head, preferred_element_type=jnp.float32)
        turns = [turn(scaled, at * QUARTER) for at in range(4)]
        wide_part = jnp.where(
            parity == 0,
            jnp.where(lane < HALF, scaled, turns[2]),
            jnp.where(lane < HALF, turns[3], turns[1]),
        )
        slim_part = jnp.where(
            parity == 0, by_quarter([turns[2], turns[3], scaled, turns[1]]), by_quarter(turns)
        )
        spread[cut, :LANES] = wide_part.astype(jnp.bfloat16)
        spread[cut, LANES:] = slim_part.astype(jnp.bfloat16)

    load_turned.wait()
    term = jnp.dot(turned[...], spread[...], preferred_element_type=jnp.float32)
    wide[:features, :] = term[:, :LANES]
    slim[:features, :] = term[:, LANES:]

    def cut_out(shard, start):
        first = start // BLOCKS
        pairs = jnp.where(pair_lane < HALF, wide[pl.ds(first, PAIRS), :], wide[pl.ds(first + PAIRS, PAIRS), :])
        quads = by_quarter([slim[pl.ds(first + at * QUADS, QUADS), :] for at in range(4)])
        out_ref[shard] = jnp.concatenate([pairs, quads], axis=0).astype(jnp.bfloat16)
        return start + counts_ref[shard] // LANES

    lax.fori_loop(0, shards, cut_out, jnp.int32(0), unroll=16)


def add_groups(terms_ref, out_ref):
    for parity in range(2):

        def add(at, total):
            return total + terms_ref[at // ROW * 2 * ROW + lax.rem(at, ROW) + parity * ROW].astype(jnp.float32)

        out_ref[parity * WINDOW : (parity + 1) * WINDOW, :] = lax.fori_loop(
            0, terms_ref.shape[0] // 2, add, jnp.zeros((WINDOW, LANES), jnp.float32), unroll=4
        )


def update_shard(place_ref, counts_ref, sums_ref, factor_ref, base_ref, out_ref, rows):
    shard = place_ref[1]
    shift = lax.rem(first_block(counts_ref, shard), BLOCKS)
    blocks = factor_ref.shape[0]

    def wide_part(head):
        pairs = sums_ref[head // 2, head % 2 * WINDOW : head % 2 * WINDOW + PAIRS, :]
        lane = WIDE[head][1]
        return jnp.concatenate([turn(pairs, lane - at * HALF) for at in range(2)], axis=0)

    def slim_part(head):
        quads = sums_ref[head // 2, head % 2 * WINDOW + PAIRS : (head % 2 + 1) * WINDOW, :]
        lane = SLIM[head][1]
        return jnp.concatenate([turn(quads, lane - at * QUARTER) for at in range(4)], axis=0)

    lane = lane_of(SPAN)
    rows[pl.ds(0, SPAN, stride=BLOCKS), :] = jnp.where(
        lane < HALF, wide_part(0), jnp.where(lane < 3 * QUARTER, slim_part(0), slim_part(1))
    )
    rows[pl.ds(1, SPAN, stride=BLOCKS), :] = jnp.where(lane < HALF, wide_part(1), wide_part(2))
    rows[pl.ds(2, SPAN, stride=BLOCKS), :] = jnp.where(
        lane < HALF, jnp.where(lane < QUARTER, slim_part(2), slim_part(3)), wide_part(3)
    )
    inner = lax.broadcasted_iota(jnp.int32, (blocks, LANES), 0)
    product = jnp.where(inner < counts_ref[shard] // LANES, rows[pl.ds(shift, blocks), :], 0.0)
    updated = base_ref[...] + factor_ref[...] * product
    for block in range(blocks):
        out_ref[0:1, block * LANES : (block + 1) * LANES] = updated[block : block + 1, :]


def call(kernel, outs, specs, operands, mebibytes, scratch=(), in_hbm=0):
    shapes = [
        (pltpu.HBM if at < in_hbm else jax.ShapeDtypeStruct)(shape, dtype) for at, (shape, dtype) in enumerate(outs)
    ]
    specs = specs + [VMEM] * (len(operands) - len(specs))
    operands = [
        pltpu.with_memory_space_constraint(operand, pltpu.HBM) if spec is HBM else operand
        for spec, operand in zip(specs, operands)
    ]
    result = pl.pallas_call(
        kernel,
        out_shape=shapes,
        in_specs=specs,
        out_specs=[HBM] * in_hbm + [VMEM] * (len(shapes) - in_hbm),
        scratch_shapes=list(scratch),
        compiler_params=pltpu.CompilerParams(vmem_limit_bytes=mebibytes * 1024 * 1024),
        name=kernel.__name__,
    )(*operands)
    return result if len(shapes) > 1 else result[0]


def body(tokens, queries, key_rows, value_rows, cotangent, probe_shards, hess_old, shard_counts):
    length, features = tokens.shape
    half = length // 2
    packed = 2 * HEADS * HEAD
    shards = shard_counts.shape[0]
    blocks = probe_shards.shape[1] // LANES
    bf16, f32 = jnp.bfloat16, jnp.float32
    slab = pltpu.VMEM((features + SPAN, LANES), f32)
    rows = pltpu.VMEM((BLOCKS * SPAN + 8, LANES), f32)
    at = lax.axis_index("dp")
    place = jnp.stack(
        [lax.axis_index("replica"), at, at // ROW % 2, lax.axis_index("tensor") % 2]
    ).astype(jnp.int32)

    def swap_copies(array):
        return lax.ppermute(array, "replica", [(0, 1), (1, 0)])

    def swap_cores(array):
        return lax.ppermute(array, "tensor", [(one, one ^ 1) for one in range(lax.axis_size("tensor"))])

    windows, keep, to_x, to_copy = call(
        pack,
        [
            ((shards, WINDOW, LANES), bf16),
            ((length, HEADS * HEAD), bf16),
            ((half, packed + features + packed), bf16),
            ((half, features + packed), bf16),
        ],
        [SMEM] + [HBM] * 7,
        (place, shard_counts, probe_shards, tokens, queries, key_rows, value_rows, cotangent),
        12,
        (
            rows,
            pltpu.SMEM(shard_counts.shape, jnp.int32),
            pltpu.VMEM(probe_shards.shape, bf16),
            pltpu.VMEM((shards, WINDOW, LANES), bf16),
            pltpu.VMEM((HEADS, *queries.shape), bf16),
            pltpu.SemaphoreType.DMA((9,)),
        ),
        in_hbm=1,
    )
    from_x = lax.ppermute(to_x, "dp", [(one, one ^ ROW) for one in range(shards)])
    from_copy = swap_copies(to_copy)

    pieces = lax.all_to_all(windows, "dp", 0, 0)

    relayed = swap_copies(from_x[:, packed:])
    swapped = swap_cores(
        jnp.concatenate([from_x[:, packed : packed + features], from_copy[:, :features]], axis=0)
    )
    swapped_last = swap_cores(relayed[:, :features])

    square = ((3, length, length), f32)
    update_part = ((blocks, LANES), f32)
    all_tokens, all_turned, *parts, factor, base = call(
        prepare,
        [
            ((3 * length, features), bf16),
            ((features, 3 * length), bf16),
            ((3, length, LANES), bf16),
            square,
            square,
            square,
            update_part,
            update_part,
        ],
        [SMEM, HBM, HBM, HBM],
        (place, tokens, probe_shards, hess_old, keep, from_x, from_copy, swapped),
        16,
        (
            pltpu.VMEM((3 * length, features), bf16),
            pltpu.VMEM((features, 3 * length), bf16),
            pltpu.VMEM(probe_shards.shape, bf16),
            pltpu.VMEM(hess_old.shape, f32),
            pltpu.SemaphoreType.DMA((5,)),
        ),
        in_hbm=2,
    )
    term_windows = call(
        middle_part,
        [((shards, WINDOW, LANES), bf16)],
        [SMEM, SMEM, HBM, HBM],
        (place, shard_counts, all_tokens, all_turned, pieces, relayed, swapped_last, *parts),
        24,
        (
            slab,
            slab,
            pltpu.VMEM((features, 2 * LANES), bf16),
            pltpu.VMEM((4 * length, 2 * LANES), bf16),
            pltpu.VMEM((4 * length, features), bf16),
            pltpu.VMEM((features, 4 * length), bf16),
            pltpu.SemaphoreType.DMA((2,)),
        ),
    )
    terms = lax.all_to_all(term_windows, "dp", 0, 0)
    summed = call(add_groups, [((2 * WINDOW, LANES), f32)], [], (terms,), 8)
    sums = lax.all_gather(summed, "replica", axis=0)
    return call(
        update_shard,
        [((1, blocks * LANES), f32)],
        [SMEM, SMEM],
        (place, shard_counts, sums, factor, base),
        8,
        (rows,),
    )


def solution(mesh):
    placed = (
        P(("dp", "replica"), None),
        P(("dp", "replica"), "tensor"),
        P(("dp", "replica"), "tensor"),
        P(("dp", "replica"), "tensor"),
        P(("dp", "replica"), "tensor"),
        P("tensor", "dp"),
        P("tensor", "dp"),
        P(),
    )
    return jax.shard_map(
        body, mesh=mesh, in_specs=placed, out_specs=P("tensor", "dp"), check_vma=False
    )
```

```python
import math

import jax
import jax.numpy as jnp
from jax import lax
from jax.experimental import pallas as pl
from jax.experimental.pallas import tpu as pltpu
from jax.sharding import PartitionSpec as P

HEAD = 96
LANES = 128
decay_rate = 0.99

ROW = 8

HEADS = 4

BLOCKS = 3
WIDE = ((0, 0), (1, 0), (1, 64), (2, 64))
SLIM = ((0, 64), (0, 96), (2, 0), (2, 32))
SPAN = 64
PAIRS = SPAN // 2
QUADS = SPAN // 4
WINDOW = PAIRS + QUADS
USED = 56
HALF = LANES // 2
QUARTER = LANES // 4

VMEM = pl.BlockSpec(memory_space=pltpu.VMEM)
SMEM = pl.BlockSpec(memory_space=pltpu.SMEM)
HBM = pl.BlockSpec(memory_space=pltpu.HBM)


def lane_of(rows):
    return lax.broadcasted_iota(jnp.int32, (rows, LANES), 1)


def turn(values, lanes):
    lanes = lanes % LANES
    return values if lanes == 0 else pltpu.roll(values, lanes, 1)


def first_block(counts_ref, shard):
    return lax.fori_loop(0, shard, lambda at, total: total + counts_ref[at] // LANES, jnp.int32(0))


def by_quarter(parts):
    lane = lane_of(parts[0].shape[0])
    low = jnp.where(lane < QUARTER, parts[0], parts[1])
    high = jnp.where(lane < 3 * QUARTER, parts[2], parts[3])
    return jnp.where(lane < HALF, low, high)


def pack(
    place_ref,
    counts_hbm,
    probe_hbm,
    tokens_hbm,
    query_hbm,
    key_hbm,
    value_hbm,
    cot_hbm,
    windows_hbm,
    keep_ref,
    x_ref,
    copy_ref,
    rows,
    counts_ref,
    probe_ref,
    windows,
    held,
    sems,
):
    copy, parity, core = place_ref[0], place_ref[2], place_ref[3]
    length, features = tokens_hbm.shape
    half = length // 2
    packed = 2 * HEADS * HEAD
    shard_loads = [
        pltpu.make_async_copy(counts_hbm, counts_ref, sems.at[0]),
        pltpu.make_async_copy(probe_hbm, probe_ref, sems.at[1]),
    ]
    arrays = [held.at[at] for at in range(HEADS)]
    head_loads = [
        pltpu.make_async_copy(source, target, sems.at[2 + at])
        for at, (source, target) in enumerate(zip((query_hbm, key_hbm, value_hbm, cot_hbm), arrays))
    ]
    tokens = tokens_hbm.at[pl.ds(pl.multiple_of(core * half, half), half), :]
    token_loads = [
        pltpu.make_async_copy(tokens, x_ref.at[:, pl.ds(packed, features)], sems.at[6]),
        pltpu.make_async_copy(tokens, copy_ref.at[:, pl.ds(0, features)], sems.at[7]),
    ]
    for load in shard_loads + head_loads + token_loads:
        load.start()
    rows[...] = jnp.zeros_like(rows)
    for load in shard_loads:
        load.wait()

    shift = lax.rem(first_block(counts_ref, place_ref[1]), BLOCKS)
    for block in range(probe_ref.shape[1] // LANES):
        rows[pl.ds(shift + block, 1), :] = probe_ref[0:1, block * LANES : (block + 1) * LANES].astype(jnp.float32)

    def window(head):
        block, lane = WIDE[head]
        wide = rows[pl.ds(block, SPAN, stride=BLOCKS), :]
        pairs = jnp.where(lane_of(PAIRS) < HALF, turn(wide[:PAIRS], -lane), turn(wide[PAIRS:], HALF - lane))
        block, lane = SLIM[head]
        slim = rows[pl.ds(block, SPAN, stride=BLOCKS), :]
        quads = by_quarter(
            [turn(slim[at * QUADS : (at + 1) * QUADS], at * QUARTER - lane) for at in range(4)]
        )
        return jnp.concatenate([pairs, quads], axis=0).astype(jnp.bfloat16)

    for which in range(2):

        @pl.when(copy == which)
        def _():
            even, odd = window(2 * which), window(2 * which + 1)

            def store(at, carry):
                first = at // ROW * 2 * ROW + lax.rem(at, ROW)
                windows[first] = even
                windows[first + ROW] = odd
                return carry

            lax.fori_loop(0, windows.shape[0] // 2, store, 0, unroll=4)

    leave = pltpu.make_async_copy(windows, windows_hbm, sems.at[8])
    leave.start()
    for load in head_loads:
        load.wait()

    def put(head, target_ref, start):
        for side in range(2):
            for at, ref in enumerate(arrays):
                to = start + (side * HEADS + at) * HEAD
                target_ref[:, to : to + HEAD] = ref[side * half : (side + 1) * half, head * HEAD : (head + 1) * HEAD]

    for mine in range(HEADS):

        @pl.when(2 * copy + parity == mine)
        def _():
            for at, ref in enumerate(arrays):
                keep_ref[:, at * HEAD : (at + 1) * HEAD] = ref[:, mine * HEAD : (mine + 1) * HEAD]
            put(mine ^ 1, x_ref, 0)
            put(mine ^ 3, x_ref, packed + features)
            put(mine ^ 2, copy_ref, features)

    for load in token_loads:
        load.wait()
    leave.wait()


def attention_part(heads):
    length = heads.shape[0]
    query, key_head, value_head, cot_head = (heads[:, at * HEAD : (at + 1) * HEAD] for at in range(HEADS))
    inv_root = 1.0 / math.sqrt(HEAD)
    causal = lax.broadcasted_iota(jnp.int32, (length, length), 0) >= lax.broadcasted_iota(
        jnp.int32, (length, length), 1
    )
    scores = inv_root * times_transposed(query, key_head)
    scores = jnp.where(causal, scores, jnp.float32(-1e30))
    expo_terms = jnp.exp(scores - jnp.max(scores, axis=1, keepdims=True))
    attn = expo_terms / jnp.sum(expo_terms, axis=1, keepdims=True)
    back = times_transposed(cot_head, value_head)
    padded_key = jnp.concatenate([key_head, jnp.zeros((length, LANES - HEAD), key_head.dtype)], axis=1)
    return padded_key, attn, back, back - jnp.sum(attn * back, axis=1, keepdims=True)


def times_transposed(left, right):
    return lax.dot_general(left, right, (((1,), (1,)), ((), ())), preferred_element_type=jnp.float32)


def join_halves(core, mine_ref, mine_at, heads_at, other_ref, other_row, tokens_ref, row):
    half, features = mine_ref.shape[0], tokens_ref.shape[1]
    side = HEADS * HEAD
    tokens_ref[pl.ds(pl.multiple_of(row + core * half, half), half), :] = mine_ref[:, mine_at : mine_at + features]
    tokens_ref[pl.ds(pl.multiple_of(row + (1 - core) * half, half), half), :] = other_ref[
        other_row : other_row + half, :
    ]
    return jnp.concatenate(
        [mine_ref[:, heads_at : heads_at + side], mine_ref[:, heads_at + side : heads_at + 2 * side]], axis=0
    )


def prepare(
    place_ref,
    tokens_hbm,
    probe_hbm,
    hess_hbm,
    keep_ref,
    x_ref,
    copy_ref,
    swapped_ref,
    tokens_out,
    turned_out,
    key_ref,
    attn_ref,
    back_ref,
    centred_ref,
    factor_ref,
    base_ref,
    tokens_ref,
    turned_ref,
    probe_ref,
    hess_ref,
    sems,
):
    core = place_ref[3]
    length, features = tokens_hbm.shape
    packed = 2 * HEADS * HEAD
    loads = [
        pltpu.make_async_copy(tokens_hbm, tokens_ref.at[pl.ds(0, length), :], sems.at[0]),
        pltpu.make_async_copy(probe_hbm, probe_ref, sems.at[1]),
        pltpu.make_async_copy(hess_hbm, hess_ref, sems.at[2]),
    ]
    for load in loads:
        load.start()
    heads_of = [
        keep_ref[...],
        join_halves(core, x_ref, packed, 0, swapped_ref, 0, tokens_ref, length),
        join_halves(core, copy_ref, 0, features, swapped_ref, x_ref.shape[0], tokens_ref, 2 * length),
    ]
    loads[0].wait()
    stores = [
        pltpu.make_async_copy(tokens_ref, tokens_out, sems.at[3]),
        pltpu.make_async_copy(turned_ref, turned_out, sems.at[4]),
    ]
    stores[0].start()
    turned_ref[...] = tokens_ref[...].T
    stores[1].start()
    for at, heads in enumerate(heads_of):
        key_ref[at], attn_ref[at], back_ref[at], centred_ref[at] = attention_part(heads)
    for load in loads[1:]:
        load.wait()
    for block in range(probe_ref.shape[1] // LANES):
        lanes = slice(block * LANES, (block + 1) * LANES)
        factor_ref[block : block + 1, :] = (1.0 - decay_rate) * probe_ref[0:1, lanes].astype(jnp.float32)
        base_ref[block : block + 1, :] = decay_rate * hess_ref[0:1, lanes]
    for store in stores:
        store.wait()


def middle_part(
    place_ref,
    counts_ref,
    tokens_hbm,
    turned_hbm,
    pieces_ref,
    relay_ref,
    swapped_ref,
    key_ref,
    attn_ref,
    back_ref,
    centred_ref,
    out_ref,
    wide,
    slim,
    probe,
    spread,
    tokens,
    turned,
    sems,
):
    last = tokens_hbm.shape[0]
    load_tokens = pltpu.make_async_copy(tokens_hbm, tokens.at[pl.ds(0, last), :], sems.at[0])
    load_turned = pltpu.make_async_copy(turned_hbm, turned.at[:, pl.ds(0, last)], sems.at[1])
    load_tokens.start()
    copy, parity, core = place_ref[0], place_ref[2], place_ref[3]
    length = attn_ref.shape[1]
    features = probe.shape[0]
    shards = pieces_ref.shape[0]
    inv_root = 1.0 / math.sqrt(HEAD)
    pair_lane, quad_lane = lane_of(PAIRS), lane_of(QUADS)
    top_row = lax.broadcasted_iota(jnp.int32, (8, LANES), 0) == 0
    wide_block = (2 * copy + parity + 1) // 2
    slim_block = 2 * copy

    def place(shard, start):
        first = start // BLOCKS
        shift = start - first * BLOCKS
        piece = pieces_ref[shard].astype(jnp.float32)
        pairs, quads = piece[:PAIRS], piece[PAIRS:]
        wide_values = [jnp.where(pair_lane < HALF, pairs, 0.0), jnp.where(pair_lane < HALF, 0.0, pairs)]
        slim_values = [jnp.where(quad_lane // QUARTER == at, quads, 0.0) for at in range(4)]
        for slab, block, values in ((wide, wide_block, wide_values), (slim, slim_block, slim_values)):
            values = jnp.concatenate(values, axis=0)
            ours = jnp.logical_not(top_row & (block < shift))
            pltpu.store(slab.at[pl.ds(first, 8), :], values[:8], mask=ours)
            slab[pl.ds(first + 8, USED - 8), :] = values[8:USED]
        return start + counts_ref[shard] // LANES

    last_heads = join_halves(core, relay_ref, 0, features, swapped_ref, 0, tokens, last)
    turned[:, last:] = tokens[last:, :].T
    parts = [(key_ref[at], attn_ref[at], back_ref[at], centred_ref[at]) for at in range(key_ref.shape[0])]
    parts.append(attention_part(last_heads))
    lax.fori_loop(0, shards, place, jnp.int32(0), unroll=8)
    load_tokens.wait()
    load_turned.start()
    probe[:, :LANES] = wide[:features, :].astype(jnp.bfloat16)
    probe[:, LANES:] = slim[:features, :].astype(jnp.bfloat16)

    side = tokens.shape[0] // 2
    product = jnp.concatenate(
        [
            jnp.dot(tokens[at * side : (at + 1) * side, :], probe[...], preferred_element_type=jnp.float32)
            for at in range(2)
        ],
        axis=0,
    )
    wide_sum, slim_sum = product[:, :LANES], product[:, LANES:]
    wide_sum = wide_sum + turn(wide_sum, HALF)
    slim_sum = slim_sum + turn(slim_sum, HALF)
    slim_sum = slim_sum + turn(slim_sum, QUARTER)
    lane = lane_of(product.shape[0])
    tangent = jnp.where(
        parity == 0,
        jnp.where(lane < HALF, wide_sum, slim_sum),
        jnp.where(lane < QUARTER, slim_sum, turn(wide_sum, QUARTER)),
    ).astype(jnp.bfloat16)

    keys, attns, backs, centreds = zip(*parts)
    cuts = [slice(at * length, (at + 1) * length) for at in range(len(parts))]
    score_tangents = [inv_root * times_transposed(tangent[cut], key_head) for cut, key_head in zip(cuts, keys)]
    means = [jnp.sum(attn * score, axis=1, keepdims=True) for attn, score in zip(attns, score_tangents)]
    weights = [attn * (score - mean) for attn, score, mean in zip(attns, score_tangents, means)]
    deltas = [jnp.sum(weight * back, axis=1, keepdims=True) for weight, back in zip(weights, backs)]
    grads = [
        (weight * centred - attn * delta).astype(jnp.bfloat16)
        for weight, centred, attn, delta in zip(weights, centreds, attns, deltas)
    ]
    lane = lane_of(length)
    for cut, grad, key_head in zip(cuts, grads, keys):
        scaled = inv_root * jnp.dot(grad, key_head, preferred_element_type=jnp.float32)
        turns = [turn(scaled, at * QUARTER) for at in range(4)]
        wide_part = jnp.where(
            parity == 0,
            jnp.where(lane < HALF, scaled, turns[2]),
            jnp.where(lane < HALF, turns[3], turns[1]),
        )
        slim_part = jnp.where(
            parity == 0, by_quarter([turns[2], turns[3], scaled, turns[1]]), by_quarter(turns)
        )
        spread[cut, :LANES] = wide_part.astype(jnp.bfloat16)
        spread[cut, LANES:] = slim_part.astype(jnp.bfloat16)

    load_turned.wait()
    term = jnp.dot(turned[...], spread[...], preferred_element_type=jnp.float32)
    wide[:features, :] = term[:, :LANES]
    slim[:features, :] = term[:, LANES:]

    def cut_out(shard, start):
        first = start // BLOCKS
        pairs = jnp.where(pair_lane < HALF, wide[pl.ds(first, PAIRS), :], wide[pl.ds(first + PAIRS, PAIRS), :])
        quads = by_quarter([slim[pl.ds(first + at * QUADS, QUADS), :] for at in range(4)])
        out_ref[shard] = jnp.concatenate([pairs, quads], axis=0).astype(jnp.bfloat16)
        return start + counts_ref[shard] // LANES

    lax.fori_loop(0, shards, cut_out, jnp.int32(0), unroll=16)


def add_groups(terms_ref, out_ref):
    for parity in range(2):

        def add(at, total):
            return total + terms_ref[at // ROW * 2 * ROW + lax.rem(at, ROW) + parity * ROW].astype(jnp.float32)

        out_ref[parity * WINDOW : (parity + 1) * WINDOW, :] = lax.fori_loop(
            0, terms_ref.shape[0] // 2, add, jnp.zeros((WINDOW, LANES), jnp.float32), unroll=4
        )


def update_shard(place_ref, counts_ref, sums_ref, factor_ref, base_ref, out_ref, rows):
    shard = place_ref[1]
    shift = lax.rem(first_block(counts_ref, shard), BLOCKS)
    blocks = factor_ref.shape[0]

    def wide_part(head):
        pairs = sums_ref[head // 2, head % 2 * WINDOW : head % 2 * WINDOW + PAIRS, :]
        lane = WIDE[head][1]
        return jnp.concatenate([turn(pairs, lane - at * HALF) for at in range(2)], axis=0)

    def slim_part(head):
        quads = sums_ref[head // 2, head % 2 * WINDOW + PAIRS : (head % 2 + 1) * WINDOW, :]
        lane = SLIM[head][1]
        return jnp.concatenate([turn(quads, lane - at * QUARTER) for at in range(4)], axis=0)

    lane = lane_of(SPAN)
    rows[pl.ds(0, SPAN, stride=BLOCKS), :] = jnp.where(
        lane < HALF, wide_part(0), jnp.where(lane < 3 * QUARTER, slim_part(0), slim_part(1))
    )
    rows[pl.ds(1, SPAN, stride=BLOCKS), :] = jnp.where(lane < HALF, wide_part(1), wide_part(2))
    rows[pl.ds(2, SPAN, stride=BLOCKS), :] = jnp.where(
        lane < HALF, jnp.where(lane < QUARTER, slim_part(2), slim_part(3)), wide_part(3)
    )
    inner = lax.broadcasted_iota(jnp.int32, (blocks, LANES), 0)
    product = jnp.where(inner < counts_ref[shard] // LANES, rows[pl.ds(shift, blocks), :], 0.0)
    updated = base_ref[...] + factor_ref[...] * product
    for block in range(blocks):
        out_ref[0:1, block * LANES : (block + 1) * LANES] = updated[block : block + 1, :]


def call(kernel, outs, specs, operands, mebibytes, scratch=(), in_hbm=0):
    shapes = [
        (pltpu.HBM if at < in_hbm else jax.ShapeDtypeStruct)(shape, dtype) for at, (shape, dtype) in enumerate(outs)
    ]
    specs = specs + [VMEM] * (len(operands) - len(specs))
    operands = [
        pltpu.with_memory_space_constraint(operand, pltpu.HBM) if spec is HBM else operand
        for spec, operand in zip(specs, operands)
    ]
    result = pl.pallas_call(
        kernel,
        out_shape=shapes,
        in_specs=specs,
        out_specs=[HBM] * in_hbm + [VMEM] * (len(shapes) - in_hbm),
        scratch_shapes=list(scratch),
        compiler_params=pltpu.CompilerParams(vmem_limit_bytes=mebibytes * 1024 * 1024),
        name=kernel.__name__,
    )(*operands)
    return result if len(shapes) > 1 else result[0]


def body(tokens, queries, key_rows, value_rows, cotangent, probe_shards, hess_old, shard_counts):
    length, features = tokens.shape
    half = length // 2
    packed = 2 * HEADS * HEAD
    shards = shard_counts.shape[0]
    blocks = probe_shards.shape[1] // LANES
    bf16, f32 = jnp.bfloat16, jnp.float32
    slab = pltpu.VMEM((features + SPAN, LANES), f32)
    rows = pltpu.VMEM((BLOCKS * SPAN + 8, LANES), f32)
    at = lax.axis_index("dp")
    place = jnp.stack(
        [lax.axis_index("replica"), at, at // ROW % 2, lax.axis_index("tensor") % 2]
    ).astype(jnp.int32)

    def swap_copies(array):
        return lax.ppermute(array, "replica", [(0, 1), (1, 0)])

    def swap_cores(array):
        return lax.ppermute(array, "tensor", [(one, one ^ 1) for one in range(lax.axis_size("tensor"))])

    windows, keep, to_x, to_copy = call(
        pack,
        [
            ((shards, WINDOW, LANES), bf16),
            ((length, HEADS * HEAD), bf16),
            ((half, packed + features + packed), bf16),
            ((half, features + packed), bf16),
        ],
        [SMEM] + [HBM] * 7,
        (place, shard_counts, probe_shards, tokens, queries, key_rows, value_rows, cotangent),
        12,
        (
            rows,
            pltpu.SMEM(shard_counts.shape, jnp.int32),
            pltpu.VMEM(probe_shards.shape, bf16),
            pltpu.VMEM((shards, WINDOW, LANES), bf16),
            pltpu.VMEM((HEADS, *queries.shape), bf16),
            pltpu.SemaphoreType.DMA((9,)),
        ),
        in_hbm=1,
    )
    from_x = lax.ppermute(to_x, "dp", [(one, one ^ ROW) for one in range(shards)])
    from_copy = swap_copies(to_copy)

    pieces = lax.all_to_all(windows, "dp", 0, 0)

    relayed = swap_copies(from_x[:, packed:])
    swapped = swap_cores(
        jnp.concatenate([from_x[:, packed : packed + features], from_copy[:, :features]], axis=0)
    )
    swapped_last = swap_cores(relayed[:, :features])

    square = ((3, length, length), f32)
    update_part = ((blocks, LANES), f32)
    all_tokens, all_turned, *parts, factor, base = call(
        prepare,
        [
            ((3 * length, features), bf16),
            ((features, 3 * length), bf16),
            ((3, length, LANES), bf16),
            square,
            square,
            square,
            update_part,
            update_part,
        ],
        [SMEM, HBM, HBM, HBM],
        (place, tokens, probe_shards, hess_old, keep, from_x, from_copy, swapped),
        16,
        (
            pltpu.VMEM((3 * length, features), bf16),
            pltpu.VMEM((features, 3 * length), bf16),
            pltpu.VMEM(probe_shards.shape, bf16),
            pltpu.VMEM(hess_old.shape, f32),
            pltpu.SemaphoreType.DMA((5,)),
        ),
        in_hbm=2,
    )
    term_windows = call(
        middle_part,
        [((shards, WINDOW, LANES), bf16)],
        [SMEM, SMEM, HBM, HBM],
        (place, shard_counts, all_tokens, all_turned, pieces, relayed, swapped_last, *parts),
        24,
        (
            slab,
            slab,
            pltpu.VMEM((features, 2 * LANES), bf16),
            pltpu.VMEM((4 * length, 2 * LANES), bf16),
            pltpu.VMEM((4 * length, features), bf16),
            pltpu.VMEM((features, 4 * length), bf16),
            pltpu.SemaphoreType.DMA((2,)),
        ),
    )
    terms = lax.all_to_all(term_windows, "dp", 0, 0)
    summed = call(add_groups, [((2 * WINDOW, LANES), f32)], [], (terms,), 8)
    sums = lax.all_gather(summed, "replica", axis=0)
    return call(
        update_shard,
        [((1, blocks * LANES), f32)],
        [SMEM, SMEM],
        (place, shard_counts, sums, factor, base),
        8,
        (rows,),
    )


def solution(mesh):
    placed = (
        P(("dp", "replica"), None),
        P(("dp", "replica"), "tensor"),
        P(("dp", "replica"), "tensor"),
        P(("dp", "replica"), "tensor"),
        P(("dp", "replica"), "tensor"),
        P("tensor", "dp"),
        P("tensor", "dp"),
        P(),
    )
    return jax.shard_map(
        body, mesh=mesh, in_specs=placed, out_specs=P("tensor", "dp"), check_vma=False
    )
```

```python
import math

import jax
import jax.numpy as jnp
from jax import lax
from jax.experimental import pallas as pl
from jax.experimental.pallas import tpu as pltpu
from jax.sharding import PartitionSpec as P

HEAD = 96
LANES = 128
decay_rate = 0.99

ROW = 8

HEADS = 4

BLOCKS = 3
WIDE = ((0, 0), (1, 0), (1, 64), (2, 64))
SLIM = ((0, 64), (0, 96), (2, 0), (2, 32))
SPAN = 64
PAIRS = SPAN // 2
QUADS = SPAN // 4
WINDOW = PAIRS + QUADS
USED = 56
HALF = LANES // 2
QUARTER = LANES // 4

VMEM = pl.BlockSpec(memory_space=pltpu.VMEM)
SMEM = pl.BlockSpec(memory_space=pltpu.SMEM)
HBM = pl.BlockSpec(memory_space=pltpu.HBM)


def lane_of(rows):
    return lax.broadcasted_iota(jnp.int32, (rows, LANES), 1)


def turn(values, lanes):
    lanes = lanes % LANES
    return values if lanes == 0 else pltpu.roll(values, lanes, 1)


def first_block(counts_ref, shard):
    return lax.fori_loop(0, shard, lambda at, total: total + counts_ref[at] // LANES, jnp.int32(0))


def by_quarter(parts):
    lane = lane_of(parts[0].shape[0])
    low = jnp.where(lane < QUARTER, parts[0], parts[1])
    high = jnp.where(lane < 3 * QUARTER, parts[2], parts[3])
    return jnp.where(lane < HALF, low, high)


def pack(
    place_ref,
    counts_hbm,
    probe_hbm,
    tokens_hbm,
    query_hbm,
    key_hbm,
    value_hbm,
    cot_hbm,
    windows_hbm,
    keep_ref,
    x_ref,
    copy_ref,
    rows,
    counts_ref,
    probe_ref,
    windows,
    held,
    sems,
):
    copy, parity, core = place_ref[0], place_ref[2], place_ref[3]
    length, features = tokens_hbm.shape
    half = length // 2
    packed = 2 * HEADS * HEAD
    shard_loads = [
        pltpu.make_async_copy(counts_hbm, counts_ref, sems.at[0]),
        pltpu.make_async_copy(probe_hbm, probe_ref, sems.at[1]),
    ]
    arrays = [held.at[at] for at in range(HEADS)]
    head_loads = [
        pltpu.make_async_copy(source, target, sems.at[2 + at])
        for at, (source, target) in enumerate(zip((query_hbm, key_hbm, value_hbm, cot_hbm), arrays))
    ]
    tokens = tokens_hbm.at[pl.ds(pl.multiple_of(core * half, half), half), :]
    token_loads = [
        pltpu.make_async_copy(tokens, x_ref.at[:, pl.ds(packed, features)], sems.at[6]),
        pltpu.make_async_copy(tokens, copy_ref.at[:, pl.ds(0, features)], sems.at[7]),
    ]
    for load in shard_loads + head_loads + token_loads:
        load.start()
    rows[...] = jnp.zeros_like(rows)
    for load in shard_loads:
        load.wait()

    shift = lax.rem(first_block(counts_ref, place_ref[1]), BLOCKS)
    for block in range(probe_ref.shape[1] // LANES):
        rows[pl.ds(shift + block, 1), :] = probe_ref[0:1, block * LANES : (block + 1) * LANES].astype(jnp.float32)

    def window(head):
        block, lane = WIDE[head]
        wide = rows[pl.ds(block, SPAN, stride=BLOCKS), :]
        pairs = jnp.where(lane_of(PAIRS) < HALF, turn(wide[:PAIRS], -lane), turn(wide[PAIRS:], HALF - lane))
        block, lane = SLIM[head]
        slim = rows[pl.ds(block, SPAN, stride=BLOCKS), :]
        quads = by_quarter(
            [turn(slim[at * QUADS : (at + 1) * QUADS], at * QUARTER - lane) for at in range(4)]
        )
        return jnp.concatenate([pairs, quads], axis=0).astype(jnp.bfloat16)

    for which in range(2):

        @pl.when(copy == which)
        def _():
            even, odd = window(2 * which), window(2 * which + 1)

            def store(at, carry):
                first = at // ROW * 2 * ROW + lax.rem(at, ROW)
                windows[first] = even
                windows[first + ROW] = odd
                return carry

            lax.fori_loop(0, windows.shape[0] // 2, store, 0, unroll=4)

    leave = pltpu.make_async_copy(windows, windows_hbm, sems.at[8])
    leave.start()
    for load in head_loads:
        load.wait()

    def put(head, target_ref, start):
        for side in range(2):
            for at, ref in enumerate(arrays):
                to = start + (side * HEADS + at) * HEAD
                target_ref[:, to : to + HEAD] = ref[side * half : (side + 1) * half, head * HEAD : (head + 1) * HEAD]

    for mine in range(HEADS):

        @pl.when(2 * copy + parity == mine)
        def _():
            for at, ref in enumerate(arrays):
                keep_ref[:, at * HEAD : (at + 1) * HEAD] = ref[:, mine * HEAD : (mine + 1) * HEAD]
            put(mine ^ 1, x_ref, 0)
            put(mine ^ 3, x_ref, packed + features)
            put(mine ^ 2, copy_ref, features)

    for load in token_loads:
        load.wait()
    leave.wait()


def attention_part(heads):
    length = heads.shape[0]
    query, key_head, value_head, cot_head = (heads[:, at * HEAD : (at + 1) * HEAD] for at in range(HEADS))
    inv_root = 1.0 / math.sqrt(HEAD)
    causal = lax.broadcasted_iota(jnp.int32, (length, length), 0) >= lax.broadcasted_iota(
        jnp.int32, (length, length), 1
    )
    scores = inv_root * times_transposed(query, key_head)
    scores = jnp.where(causal, scores, jnp.float32(-1e30))
    expo_terms = jnp.exp(scores - jnp.max(scores, axis=1, keepdims=True))
    attn = expo_terms / jnp.sum(expo_terms, axis=1, keepdims=True)
    back = times_transposed(cot_head, value_head)
    padded_key = jnp.concatenate([key_head, jnp.zeros((length, LANES - HEAD), key_head.dtype)], axis=1)
    return padded_key, attn, back, back - jnp.sum(attn * back, axis=1, keepdims=True)


def times_transposed(left, right):
    return lax.dot_general(left, right, (((1,), (1,)), ((), ())), preferred_element_type=jnp.float32)


def join_halves(core, mine_ref, mine_at, heads_at, other_ref, other_row, tokens_ref, row):
    half, features = mine_ref.shape[0], tokens_ref.shape[1]
    side = HEADS * HEAD
    tokens_ref[pl.ds(pl.multiple_of(row + core * half, half), half), :] = mine_ref[:, mine_at : mine_at + features]
    tokens_ref[pl.ds(pl.multiple_of(row + (1 - core) * half, half), half), :] = other_ref[
        other_row : other_row + half, :
    ]
    return jnp.concatenate(
        [mine_ref[:, heads_at : heads_at + side], mine_ref[:, heads_at + side : heads_at + 2 * side]], axis=0
    )


def prepare(
    place_ref,
    tokens_hbm,
    probe_hbm,
    hess_hbm,
    keep_ref,
    x_ref,
    copy_ref,
    swapped_ref,
    tokens_out,
    turned_out,
    factor_out,
    base_out,
    key_ref,
    attn_ref,
    back_ref,
    centred_ref,
    tokens_ref,
    turned_ref,
    factor_ref,
    base_ref,
    probe_ref,
    hess_ref,
    sems,
):
    core = place_ref[3]
    length, features = tokens_hbm.shape
    packed = 2 * HEADS * HEAD
    loads = [
        pltpu.make_async_copy(tokens_hbm, tokens_ref.at[pl.ds(0, length), :], sems.at[0]),
        pltpu.make_async_copy(probe_hbm, probe_ref, sems.at[1]),
        pltpu.make_async_copy(hess_hbm, hess_ref, sems.at[2]),
    ]
    for load in loads:
        load.start()
    heads_of = [
        keep_ref[...],
        join_halves(core, x_ref, packed, 0, swapped_ref, 0, tokens_ref, length),
        join_halves(core, copy_ref, 0, features, swapped_ref, x_ref.shape[0], tokens_ref, 2 * length),
    ]
    loads[0].wait()
    stores = [
        pltpu.make_async_copy(tokens_ref, tokens_out, sems.at[3]),
        pltpu.make_async_copy(turned_ref, turned_out, sems.at[4]),
        pltpu.make_async_copy(factor_ref, factor_out, sems.at[5]),
        pltpu.make_async_copy(base_ref, base_out, sems.at[6]),
    ]
    stores[0].start()
    turned_ref[...] = tokens_ref[...].T
    stores[1].start()
    for load in loads[1:]:
        load.wait()
    for block in range(probe_ref.shape[1] // LANES):
        lanes = slice(block * LANES, (block + 1) * LANES)
        factor_ref[block : block + 1, :] = (1.0 - decay_rate) * probe_ref[0:1, lanes].astype(jnp.float32)
        base_ref[block : block + 1, :] = decay_rate * hess_ref[0:1, lanes]
    for store in stores[2:]:
        store.start()
    for at, heads in enumerate(heads_of):
        key_ref[at], attn_ref[at], back_ref[at], centred_ref[at] = attention_part(heads)
    for store in stores:
        store.wait()


def middle_part(
    place_ref,
    counts_ref,
    tokens_hbm,
    turned_hbm,
    pieces_ref,
    relay_ref,
    swapped_ref,
    key_ref,
    attn_ref,
    back_ref,
    centred_ref,
    out_ref,
    wide,
    slim,
    probe,
    spread,
    tokens,
    turned,
    sems,
):
    last = tokens_hbm.shape[0]
    load_tokens = pltpu.make_async_copy(tokens_hbm, tokens.at[pl.ds(0, last), :], sems.at[0])
    load_turned = pltpu.make_async_copy(turned_hbm, turned.at[:, pl.ds(0, last)], sems.at[1])
    load_tokens.start()
    copy, parity, core = place_ref[0], place_ref[2], place_ref[3]
    length = attn_ref.shape[1]
    features = probe.shape[0]
    shards = pieces_ref.shape[0]
    inv_root = 1.0 / math.sqrt(HEAD)
    pair_lane, quad_lane = lane_of(PAIRS), lane_of(QUADS)
    top_row = lax.broadcasted_iota(jnp.int32, (8, LANES), 0) == 0
    wide_block = (2 * copy + parity + 1) // 2
    slim_block = 2 * copy

    def place(shard, start):
        first = start // BLOCKS
        shift = start - first * BLOCKS
        piece = pieces_ref[shard].astype(jnp.float32)
        pairs, quads = piece[:PAIRS], piece[PAIRS:]
        wide_values = [jnp.where(pair_lane < HALF, pairs, 0.0), jnp.where(pair_lane < HALF, 0.0, pairs)]
        slim_values = [jnp.where(quad_lane // QUARTER == at, quads, 0.0) for at in range(4)]
        for slab, block, values in ((wide, wide_block, wide_values), (slim, slim_block, slim_values)):
            values = jnp.concatenate(values, axis=0)
            ours = jnp.logical_not(top_row & (block < shift))
            pltpu.store(slab.at[pl.ds(first, 8), :], values[:8], mask=ours)
            slab[pl.ds(first + 8, USED - 8), :] = values[8:USED]
        return start + counts_ref[shard] // LANES

    last_heads = join_halves(core, relay_ref, 0, features, swapped_ref, 0, tokens, last)
    turned[:, last:] = tokens[last:, :].T
    parts = [(key_ref[at], attn_ref[at], back_ref[at], centred_ref[at]) for at in range(key_ref.shape[0])]
    parts.append(attention_part(last_heads))
    lax.fori_loop(0, shards, place, jnp.int32(0), unroll=8)
    load_tokens.wait()
    load_turned.start()
    probe[:, :LANES] = wide[:features, :].astype(jnp.bfloat16)
    probe[:, LANES:] = slim[:features, :].astype(jnp.bfloat16)

    side = tokens.shape[0] // 2
    product = jnp.concatenate(
        [
            jnp.dot(tokens[at * side : (at + 1) * side, :], probe[...], preferred_element_type=jnp.float32)
            for at in range(2)
        ],
        axis=0,
    )
    wide_sum, slim_sum = product[:, :LANES], product[:, LANES:]
    wide_sum = wide_sum + turn(wide_sum, HALF)
    slim_sum = slim_sum + turn(slim_sum, HALF)
    slim_sum = slim_sum + turn(slim_sum, QUARTER)
    lane = lane_of(product.shape[0])
    tangent = jnp.where(
        parity == 0,
        jnp.where(lane < HALF, wide_sum, slim_sum),
        jnp.where(lane < QUARTER, slim_sum, turn(wide_sum, QUARTER)),
    ).astype(jnp.bfloat16)

    keys, attns, backs, centreds = zip(*parts)
    cuts = [slice(at * length, (at + 1) * length) for at in range(len(parts))]
    score_tangents = [inv_root * times_transposed(tangent[cut], key_head) for cut, key_head in zip(cuts, keys)]
    means = [jnp.sum(attn * score, axis=1, keepdims=True) for attn, score in zip(attns, score_tangents)]
    weights = [attn * (score - mean) for attn, score, mean in zip(attns, score_tangents, means)]
    deltas = [jnp.sum(weight * back, axis=1, keepdims=True) for weight, back in zip(weights, backs)]
    grads = [
        (weight * centred - attn * delta).astype(jnp.bfloat16)
        for weight, centred, attn, delta in zip(weights, centreds, attns, deltas)
    ]
    lane = lane_of(length)
    for cut, grad, key_head in zip(cuts, grads, keys):
        scaled = inv_root * jnp.dot(grad, key_head, preferred_element_type=jnp.float32)
        turns = [turn(scaled, at * QUARTER) for at in range(4)]
        wide_part = jnp.where(
            parity == 0,
            jnp.where(lane < HALF, scaled, turns[2]),
            jnp.where(lane < HALF, turns[3], turns[1]),
        )
        slim_part = jnp.where(
            parity == 0, by_quarter([turns[2], turns[3], scaled, turns[1]]), by_quarter(turns)
        )
        spread[cut, :LANES] = wide_part.astype(jnp.bfloat16)
        spread[cut, LANES:] = slim_part.astype(jnp.bfloat16)

    load_turned.wait()
    term = jnp.dot(turned[...], spread[...], preferred_element_type=jnp.float32)
    wide[:features, :] = term[:, :LANES]
    slim[:features, :] = term[:, LANES:]

    def cut_out(shard, start):
        first = start // BLOCKS
        pairs = jnp.where(pair_lane < HALF, wide[pl.ds(first, PAIRS), :], wide[pl.ds(first + PAIRS, PAIRS), :])
        quads = by_quarter([slim[pl.ds(first + at * QUADS, QUADS), :] for at in range(4)])
        out_ref[shard] = jnp.concatenate([pairs, quads], axis=0).astype(jnp.bfloat16)
        return start + counts_ref[shard] // LANES

    lax.fori_loop(0, shards, cut_out, jnp.int32(0), unroll=16)


def add_groups(terms_ref, out_ref):
    for parity in range(2):

        def add(at, total):
            return total + terms_ref[at // ROW * 2 * ROW + lax.rem(at, ROW) + parity * ROW].astype(jnp.float32)

        out_ref[parity * WINDOW : (parity + 1) * WINDOW, :] = lax.fori_loop(
            0, terms_ref.shape[0] // 2, add, jnp.zeros((WINDOW, LANES), jnp.float32), unroll=4
        )


def update_shard(place_ref, counts_ref, sums_ref, factor_ref, base_ref, out_ref, rows):
    shard = place_ref[1]
    shift = lax.rem(first_block(counts_ref, shard), BLOCKS)
    blocks = factor_ref.shape[0]

    def wide_part(head):
        pairs = sums_ref[head // 2, head % 2 * WINDOW : head % 2 * WINDOW + PAIRS, :]
        lane = WIDE[head][1]
        return jnp.concatenate([turn(pairs, lane - at * HALF) for at in range(2)], axis=0)

    def slim_part(head):
        quads = sums_ref[head // 2, head % 2 * WINDOW + PAIRS : (head % 2 + 1) * WINDOW, :]
        lane = SLIM[head][1]
        return jnp.concatenate([turn(quads, lane - at * QUARTER) for at in range(4)], axis=0)

    lane = lane_of(SPAN)
    rows[pl.ds(0, SPAN, stride=BLOCKS), :] = jnp.where(
        lane < HALF, wide_part(0), jnp.where(lane < 3 * QUARTER, slim_part(0), slim_part(1))
    )
    rows[pl.ds(1, SPAN, stride=BLOCKS), :] = jnp.where(lane < HALF, wide_part(1), wide_part(2))
    rows[pl.ds(2, SPAN, stride=BLOCKS), :] = jnp.where(
        lane < HALF, jnp.where(lane < QUARTER, slim_part(2), slim_part(3)), wide_part(3)
    )
    inner = lax.broadcasted_iota(jnp.int32, (blocks, LANES), 0)
    product = jnp.where(inner < counts_ref[shard] // LANES, rows[pl.ds(shift, blocks), :], 0.0)
    updated = base_ref[...] + factor_ref[...] * product
    for block in range(blocks):
        out_ref[0:1, block * LANES : (block + 1) * LANES] = updated[block : block + 1, :]


def call(kernel, outs, specs, operands, mebibytes, scratch=(), in_hbm=0):
    shapes = [
        (pltpu.HBM if at < in_hbm else jax.ShapeDtypeStruct)(shape, dtype) for at, (shape, dtype) in enumerate(outs)
    ]
    specs = specs + [VMEM] * (len(operands) - len(specs))
    operands = [
        pltpu.with_memory_space_constraint(operand, pltpu.HBM) if spec is HBM else operand
        for spec, operand in zip(specs, operands)
    ]
    result = pl.pallas_call(
        kernel,
        out_shape=shapes,
        in_specs=specs,
        out_specs=[HBM] * in_hbm + [VMEM] * (len(shapes) - in_hbm),
        scratch_shapes=list(scratch),
        compiler_params=pltpu.CompilerParams(vmem_limit_bytes=mebibytes * 1024 * 1024),
        name=kernel.__name__,
    )(*operands)
    return result if len(shapes) > 1 else result[0]


def body(tokens, queries, key_rows, value_rows, cotangent, probe_shards, hess_old, shard_counts):
    length, features = tokens.shape
    half = length // 2
    packed = 2 * HEADS * HEAD
    shards = shard_counts.shape[0]
    blocks = probe_shards.shape[1] // LANES
    bf16, f32 = jnp.bfloat16, jnp.float32
    slab = pltpu.VMEM((features + SPAN, LANES), f32)
    rows = pltpu.VMEM((BLOCKS * SPAN + 8, LANES), f32)
    at = lax.axis_index("dp")
    place = jnp.stack(
        [lax.axis_index("replica"), at, at // ROW % 2, lax.axis_index("tensor") % 2]
    ).astype(jnp.int32)

    def swap_copies(array):
        return lax.ppermute(array, "replica", [(0, 1), (1, 0)])

    def swap_cores(array):
        return lax.ppermute(array, "tensor", [(one, one ^ 1) for one in range(lax.axis_size("tensor"))])

    windows, keep, to_x, to_copy = call(
        pack,
        [
            ((shards, WINDOW, LANES), bf16),
            ((length, HEADS * HEAD), bf16),
            ((half, packed + features + packed), bf16),
            ((half, features + packed), bf16),
        ],
        [SMEM] + [HBM] * 7,
        (place, shard_counts, probe_shards, tokens, queries, key_rows, value_rows, cotangent),
        12,
        (
            rows,
            pltpu.SMEM(shard_counts.shape, jnp.int32),
            pltpu.VMEM(probe_shards.shape, bf16),
            pltpu.VMEM((shards, WINDOW, LANES), bf16),
            pltpu.VMEM((HEADS, *queries.shape), bf16),
            pltpu.SemaphoreType.DMA((9,)),
        ),
        in_hbm=1,
    )
    from_x = lax.ppermute(to_x, "dp", [(one, one ^ ROW) for one in range(shards)])
    from_copy = swap_copies(to_copy)

    pieces = lax.all_to_all(windows, "dp", 0, 0)

    relayed = swap_copies(from_x[:, packed:])
    swapped = swap_cores(
        jnp.concatenate([from_x[:, packed : packed + features], from_copy[:, :features]], axis=0)
    )
    square = ((3, length, length), f32)
    update_part = ((blocks, LANES), f32)
    all_tokens, all_turned, factor, base, *parts = call(
        prepare,
        [
            ((3 * length, features), bf16),
            ((features, 3 * length), bf16),
            update_part,
            update_part,
            ((3, length, LANES), bf16),
            square,
            square,
            square,
        ],
        [SMEM, HBM, HBM, HBM],
        (place, tokens, probe_shards, hess_old, keep, from_x, from_copy, swapped),
        16,
        (
            pltpu.VMEM((3 * length, features), bf16),
            pltpu.VMEM((features, 3 * length), bf16),
            pltpu.VMEM((blocks, LANES), f32),
            pltpu.VMEM((blocks, LANES), f32),
            pltpu.VMEM(probe_shards.shape, bf16),
            pltpu.VMEM(hess_old.shape, f32),
            pltpu.SemaphoreType.DMA((7,)),
        ),
        in_hbm=4,
    )
    swapped_last = swap_cores(relayed[:, :features])
    term_windows = call(
        middle_part,
        [((shards, WINDOW, LANES), bf16)],
        [SMEM, SMEM, HBM, HBM],
        (place, shard_counts, all_tokens, all_turned, pieces, relayed, swapped_last, *parts),
        24,
        (
            slab,
            slab,
            pltpu.VMEM((features, 2 * LANES), bf16),
            pltpu.VMEM((4 * length, 2 * LANES), bf16),
            pltpu.VMEM((4 * length, features), bf16),
            pltpu.VMEM((features, 4 * length), bf16),
            pltpu.SemaphoreType.DMA((2,)),
        ),
    )
    terms = lax.all_to_all(term_windows, "dp", 0, 0)
    summed = call(add_groups, [((2 * WINDOW, LANES), f32)], [], (terms,), 8)
    sums = lax.all_gather(summed, "replica", axis=0)
    return call(
        update_shard,
        [((1, blocks * LANES), f32)],
        [SMEM, SMEM],
        (place, shard_counts, sums, factor, base),
        8,
        (rows,),
    )


def solution(mesh):
    placed = (
        P(("dp", "replica"), None),
        P(("dp", "replica"), "tensor"),
        P(("dp", "replica"), "tensor"),
        P(("dp", "replica"), "tensor"),
        P(("dp", "replica"), "tensor"),
        P("tensor", "dp"),
        P("tensor", "dp"),
        P(),
    )
    return jax.shard_map(
        body, mesh=mesh, in_specs=placed, out_specs=P("tensor", "dp"), check_vma=False
    )
```

```python
import math

import jax
import jax.numpy as jnp
from jax import lax
from jax.experimental import pallas as pl
from jax.experimental.pallas import tpu as pltpu
from jax.sharding import PartitionSpec as P

HEAD = 96
LANES = 128
decay_rate = 0.99

ROW = 8

HEADS = 4

BLOCKS = 3
WIDE = ((0, 0), (1, 0), (1, 64), (2, 64))
SLIM = ((0, 64), (0, 96), (2, 0), (2, 32))
SPAN = 64
PAIRS = SPAN // 2
QUADS = SPAN // 4
WINDOW = PAIRS + QUADS
USED = 56
HALF = LANES // 2
QUARTER = LANES // 4

VMEM = pl.BlockSpec(memory_space=pltpu.VMEM)
SMEM = pl.BlockSpec(memory_space=pltpu.SMEM)
HBM = pl.BlockSpec(memory_space=pltpu.HBM)


def lane_of(rows):
    return lax.broadcasted_iota(jnp.int32, (rows, LANES), 1)


def turn(values, lanes):
    lanes = lanes % LANES
    return values if lanes == 0 else pltpu.roll(values, lanes, 1)


def first_block(counts_ref, shard):
    return lax.fori_loop(0, shard, lambda at, total: total + counts_ref[at] // LANES, jnp.int32(0))


def by_quarter(parts):
    lane = lane_of(parts[0].shape[0])
    low = jnp.where(lane < QUARTER, parts[0], parts[1])
    high = jnp.where(lane < 3 * QUARTER, parts[2], parts[3])
    return jnp.where(lane < HALF, low, high)


def pack(
    place_ref,
    counts_hbm,
    probe_hbm,
    tokens_hbm,
    query_hbm,
    key_hbm,
    value_hbm,
    cot_hbm,
    windows_hbm,
    keep_ref,
    x_ref,
    copy_ref,
    rows,
    counts_ref,
    probe_ref,
    windows,
    held,
    sems,
):
    copy, parity, core = place_ref[0], place_ref[2], place_ref[3]
    length, features = tokens_hbm.shape
    half = length // 2
    packed = 2 * HEADS * HEAD
    shard_loads = [
        pltpu.make_async_copy(counts_hbm, counts_ref, sems.at[0]),
        pltpu.make_async_copy(probe_hbm, probe_ref, sems.at[1]),
    ]
    arrays = [held.at[at] for at in range(HEADS)]
    head_loads = [
        pltpu.make_async_copy(source, target, sems.at[2 + at])
        for at, (source, target) in enumerate(zip((query_hbm, key_hbm, value_hbm, cot_hbm), arrays))
    ]
    tokens = tokens_hbm.at[pl.ds(pl.multiple_of(core * half, half), half), :]
    token_loads = [
        pltpu.make_async_copy(tokens, x_ref.at[:, pl.ds(packed, features)], sems.at[6]),
        pltpu.make_async_copy(tokens, copy_ref.at[:, pl.ds(0, features)], sems.at[7]),
    ]
    for load in shard_loads + head_loads + token_loads:
        load.start()
    rows[...] = jnp.zeros_like(rows)
    for load in shard_loads:
        load.wait()

    shift = lax.rem(first_block(counts_ref, place_ref[1]), BLOCKS)
    for block in range(probe_ref.shape[1] // LANES):
        rows[pl.ds(shift + block, 1), :] = probe_ref[0:1, block * LANES : (block + 1) * LANES].astype(jnp.float32)

    def window(head):
        block, lane = WIDE[head]
        wide = rows[pl.ds(block, SPAN, stride=BLOCKS), :]
        pairs = jnp.where(lane_of(PAIRS) < HALF, turn(wide[:PAIRS], -lane), turn(wide[PAIRS:], HALF - lane))
        block, lane = SLIM[head]
        slim = rows[pl.ds(block, SPAN, stride=BLOCKS), :]
        quads = by_quarter(
            [turn(slim[at * QUADS : (at + 1) * QUADS], at * QUARTER - lane) for at in range(4)]
        )
        return jnp.concatenate([pairs, quads], axis=0).astype(jnp.bfloat16)

    for which in range(2):

        @pl.when(copy == which)
        def _():
            even, odd = window(2 * which), window(2 * which + 1)

            def store(at, carry):
                first = at // ROW * 2 * ROW + lax.rem(at, ROW)
                windows[first] = even
                windows[first + ROW] = odd
                return carry

            lax.fori_loop(0, windows.shape[0] // 2, store, 0, unroll=4)

    leave = pltpu.make_async_copy(windows, windows_hbm, sems.at[8])
    leave.start()
    for load in head_loads:
        load.wait()

    def put(head, target_ref, start):
        for side in range(2):
            for at, ref in enumerate(arrays):
                to = start + (side * HEADS + at) * HEAD
                target_ref[:, to : to + HEAD] = ref[side * half : (side + 1) * half, head * HEAD : (head + 1) * HEAD]

    for mine in range(HEADS):

        @pl.when(2 * copy + parity == mine)
        def _():
            for at, ref in enumerate(arrays):
                keep_ref[:, at * HEAD : (at + 1) * HEAD] = ref[:, mine * HEAD : (mine + 1) * HEAD]
            put(mine ^ 1, x_ref, 0)
            put(mine ^ 3, x_ref, packed + features)
            put(mine ^ 2, copy_ref, features)

    for load in token_loads:
        load.wait()
    leave.wait()


def attention_part(heads):
    length = heads.shape[0]
    query, key_head, value_head, cot_head = (heads[:, at * HEAD : (at + 1) * HEAD] for at in range(HEADS))
    inv_root = 1.0 / math.sqrt(HEAD)
    causal = lax.broadcasted_iota(jnp.int32, (length, length), 0) >= lax.broadcasted_iota(
        jnp.int32, (length, length), 1
    )
    scores = inv_root * times_transposed(query, key_head)
    scores = jnp.where(causal, scores, jnp.float32(-1e30))
    expo_terms = jnp.exp(scores - jnp.max(scores, axis=1, keepdims=True))
    attn = expo_terms / jnp.sum(expo_terms, axis=1, keepdims=True)
    back = times_transposed(cot_head, value_head)
    padded_key = jnp.concatenate([key_head, jnp.zeros((length, LANES - HEAD), key_head.dtype)], axis=1)
    return padded_key, attn, back, back - jnp.sum(attn * back, axis=1, keepdims=True)


def times_transposed(left, right):
    return lax.dot_general(left, right, (((1,), (1,)), ((), ())), preferred_element_type=jnp.float32)


def join_halves(core, mine_ref, mine_at, heads_at, other_ref, other_row, tokens_ref, row):
    half, features = mine_ref.shape[0], tokens_ref.shape[1]
    side = HEADS * HEAD
    tokens_ref[pl.ds(pl.multiple_of(row + core * half, half), half), :] = mine_ref[:, mine_at : mine_at + features]
    tokens_ref[pl.ds(pl.multiple_of(row + (1 - core) * half, half), half), :] = other_ref[
        other_row : other_row + half, :
    ]
    return jnp.concatenate(
        [mine_ref[:, heads_at : heads_at + side], mine_ref[:, heads_at + side : heads_at + 2 * side]], axis=0
    )


def prepare(
    place_ref,
    tokens_hbm,
    probe_hbm,
    hess_hbm,
    keep_ref,
    x_ref,
    copy_ref,
    swapped_ref,
    tokens_out,
    turned_out,
    factor_out,
    base_out,
    key_ref,
    attn_ref,
    back_ref,
    centred_ref,
    tokens_ref,
    turned_ref,
    factor_ref,
    base_ref,
    probe_ref,
    hess_ref,
    sems,
):
    core = place_ref[3]
    length, features = tokens_hbm.shape
    packed = 2 * HEADS * HEAD
    loads = [
        pltpu.make_async_copy(tokens_hbm, tokens_ref.at[pl.ds(0, length), :], sems.at[0]),
        pltpu.make_async_copy(probe_hbm, probe_ref, sems.at[1]),
        pltpu.make_async_copy(hess_hbm, hess_ref, sems.at[2]),
    ]
    for load in loads:
        load.start()
    heads_of = [
        keep_ref[...],
        join_halves(core, x_ref, packed, 0, swapped_ref, 0, tokens_ref, length),
        join_halves(core, copy_ref, 0, features, swapped_ref, x_ref.shape[0], tokens_ref, 2 * length),
    ]
    key_ref[0], attn_ref[0], back_ref[0], centred_ref[0] = attention_part(heads_of[0])
    loads[0].wait()
    stores = [
        pltpu.make_async_copy(tokens_ref, tokens_out, sems.at[3]),
        pltpu.make_async_copy(turned_ref, turned_out, sems.at[4]),
        pltpu.make_async_copy(factor_ref, factor_out, sems.at[5]),
        pltpu.make_async_copy(base_ref, base_out, sems.at[6]),
    ]
    stores[0].start()
    turned_ref[...] = tokens_ref[...].T
    stores[1].start()
    for load in loads[1:]:
        load.wait()
    for block in range(probe_ref.shape[1] // LANES):
        lanes = slice(block * LANES, (block + 1) * LANES)
        factor_ref[block : block + 1, :] = (1.0 - decay_rate) * probe_ref[0:1, lanes].astype(jnp.float32)
        base_ref[block : block + 1, :] = decay_rate * hess_ref[0:1, lanes]
    for store in stores[2:]:
        store.start()
    for at, heads in list(enumerate(heads_of))[1:]:
        key_ref[at], attn_ref[at], back_ref[at], centred_ref[at] = attention_part(heads)
    for store in stores:
        store.wait()


def middle_part(
    place_ref,
    counts_ref,
    tokens_hbm,
    turned_hbm,
    pieces_ref,
    relay_ref,
    swapped_ref,
    key_ref,
    attn_ref,
    back_ref,
    centred_ref,
    out_ref,
    wide,
    slim,
    probe,
    spread,
    tokens,
    turned,
    sems,
):
    last = tokens_hbm.shape[0]
    load_tokens = pltpu.make_async_copy(tokens_hbm, tokens.at[pl.ds(0, last), :], sems.at[0])
    load_turned = pltpu.make_async_copy(turned_hbm, turned.at[:, pl.ds(0, last)], sems.at[1])
    load_tokens.start()
    copy, parity, core = place_ref[0], place_ref[2], place_ref[3]
    length = attn_ref.shape[1]
    features = probe.shape[0]
    shards = pieces_ref.shape[0]
    inv_root = 1.0 / math.sqrt(HEAD)
    pair_lane, quad_lane = lane_of(PAIRS), lane_of(QUADS)
    top_row = lax.broadcasted_iota(jnp.int32, (8, LANES), 0) == 0
    wide_block = (2 * copy + parity + 1) // 2
    slim_block = 2 * copy

    def place(shard, start):
        first = start // BLOCKS
        shift = start - first * BLOCKS
        piece = pieces_ref[shard].astype(jnp.float32)
        pairs, quads = piece[:PAIRS], piece[PAIRS:]
        wide_values = [jnp.where(pair_lane < HALF, pairs, 0.0), jnp.where(pair_lane < HALF, 0.0, pairs)]
        slim_values = [jnp.where(quad_lane // QUARTER == at, quads, 0.0) for at in range(4)]
        for slab, block, values in ((wide, wide_block, wide_values), (slim, slim_block, slim_values)):
            values = jnp.concatenate(values, axis=0)
            ours = jnp.logical_not(top_row & (block < shift))
            pltpu.store(slab.at[pl.ds(first, 8), :], values[:8], mask=ours)
            slab[pl.ds(first + 8, USED - 8), :] = values[8:USED]
        return start + counts_ref[shard] // LANES

    last_heads = join_halves(core, relay_ref, 0, features, swapped_ref, 0, tokens, last)
    turned[:, last:] = tokens[last:, :].T
    parts = [(key_ref[at], attn_ref[at], back_ref[at], centred_ref[at]) for at in range(key_ref.shape[0])]
    parts.append(attention_part(last_heads))
    lax.fori_loop(0, shards, place, jnp.int32(0), unroll=8)
    load_tokens.wait()
    load_turned.start()
    probe[:, :LANES] = wide[:features, :].astype(jnp.bfloat16)
    probe[:, LANES:] = slim[:features, :].astype(jnp.bfloat16)

    side = tokens.shape[0] // 2
    product = jnp.concatenate(
        [
            jnp.dot(tokens[at * side : (at + 1) * side, :], probe[...], preferred_element_type=jnp.float32)
            for at in range(2)
        ],
        axis=0,
    )
    wide_sum, slim_sum = product[:, :LANES], product[:, LANES:]
    wide_sum = wide_sum + turn(wide_sum, HALF)
    slim_sum = slim_sum + turn(slim_sum, HALF)
    slim_sum = slim_sum + turn(slim_sum, QUARTER)
    lane = lane_of(product.shape[0])
    tangent = jnp.where(
        parity == 0,
        jnp.where(lane < HALF, wide_sum, slim_sum),
        jnp.where(lane < QUARTER, slim_sum, turn(wide_sum, QUARTER)),
    ).astype(jnp.bfloat16)

    keys, attns, backs, centreds = zip(*parts)
    cuts = [slice(at * length, (at + 1) * length) for at in range(len(parts))]
    score_tangents = [inv_root * times_transposed(tangent[cut], key_head) for cut, key_head in zip(cuts, keys)]
    means = [jnp.sum(attn * score, axis=1, keepdims=True) for attn, score in zip(attns, score_tangents)]
    weights = [attn * (score - mean) for attn, score, mean in zip(attns, score_tangents, means)]
    deltas = [jnp.sum(weight * back, axis=1, keepdims=True) for weight, back in zip(weights, backs)]
    grads = [
        (weight * centred - attn * delta).astype(jnp.bfloat16)
        for weight, centred, attn, delta in zip(weights, centreds, attns, deltas)
    ]
    lane = lane_of(length)
    for cut, grad, key_head in zip(cuts, grads, keys):
        scaled = inv_root * jnp.dot(grad, key_head, preferred_element_type=jnp.float32)
        turns = [turn(scaled, at * QUARTER) for at in range(4)]
        wide_part = jnp.where(
            parity == 0,
            jnp.where(lane < HALF, scaled, turns[2]),
            jnp.where(lane < HALF, turns[3], turns[1]),
        )
        slim_part = jnp.where(
            parity == 0, by_quarter([turns[2], turns[3], scaled, turns[1]]), by_quarter(turns)
        )
        spread[cut, :LANES] = wide_part.astype(jnp.bfloat16)
        spread[cut, LANES:] = slim_part.astype(jnp.bfloat16)

    load_turned.wait()
    term = jnp.dot(turned[...], spread[...], preferred_element_type=jnp.float32)
    wide[:features, :] = term[:, :LANES]
    slim[:features, :] = term[:, LANES:]

    def cut_out(shard, start):
        first = start // BLOCKS
        pairs = jnp.where(pair_lane < HALF, wide[pl.ds(first, PAIRS), :], wide[pl.ds(first + PAIRS, PAIRS), :])
        quads = by_quarter([slim[pl.ds(first + at * QUADS, QUADS), :] for at in range(4)])
        out_ref[shard] = jnp.concatenate([pairs, quads], axis=0).astype(jnp.bfloat16)
        return start + counts_ref[shard] // LANES

    lax.fori_loop(0, shards, cut_out, jnp.int32(0), unroll=16)


def add_groups(terms_ref, out_ref):
    for parity in range(2):

        def add(at, total):
            return total + terms_ref[at // ROW * 2 * ROW + lax.rem(at, ROW) + parity * ROW].astype(jnp.float32)

        out_ref[parity * WINDOW : (parity + 1) * WINDOW, :] = lax.fori_loop(
            0, terms_ref.shape[0] // 2, add, jnp.zeros((WINDOW, LANES), jnp.float32), unroll=4
        )


def update_shard(place_ref, counts_ref, sums_ref, factor_ref, base_ref, out_ref, rows):
    shard = place_ref[1]
    shift = lax.rem(first_block(counts_ref, shard), BLOCKS)
    blocks = factor_ref.shape[0]

    def wide_part(head):
        pairs = sums_ref[head // 2, head % 2 * WINDOW : head % 2 * WINDOW + PAIRS, :]
        lane = WIDE[head][1]
        return jnp.concatenate([turn(pairs, lane - at * HALF) for at in range(2)], axis=0)

    def slim_part(head):
        quads = sums_ref[head // 2, head % 2 * WINDOW + PAIRS : (head % 2 + 1) * WINDOW, :]
        lane = SLIM[head][1]
        return jnp.concatenate([turn(quads, lane - at * QUARTER) for at in range(4)], axis=0)

    lane = lane_of(SPAN)
    rows[pl.ds(0, SPAN, stride=BLOCKS), :] = jnp.where(
        lane < HALF, wide_part(0), jnp.where(lane < 3 * QUARTER, slim_part(0), slim_part(1))
    )
    rows[pl.ds(1, SPAN, stride=BLOCKS), :] = jnp.where(lane < HALF, wide_part(1), wide_part(2))
    rows[pl.ds(2, SPAN, stride=BLOCKS), :] = jnp.where(
        lane < HALF, jnp.where(lane < QUARTER, slim_part(2), slim_part(3)), wide_part(3)
    )
    inner = lax.broadcasted_iota(jnp.int32, (blocks, LANES), 0)
    product = jnp.where(inner < counts_ref[shard] // LANES, rows[pl.ds(shift, blocks), :], 0.0)
    updated = base_ref[...] + factor_ref[...] * product
    for block in range(blocks):
        out_ref[0:1, block * LANES : (block + 1) * LANES] = updated[block : block + 1, :]


def call(kernel, outs, specs, operands, mebibytes, scratch=(), in_hbm=0):
    shapes = [
        (pltpu.HBM if at < in_hbm else jax.ShapeDtypeStruct)(shape, dtype) for at, (shape, dtype) in enumerate(outs)
    ]
    specs = specs + [VMEM] * (len(operands) - len(specs))
    operands = [
        pltpu.with_memory_space_constraint(operand, pltpu.HBM) if spec is HBM else operand
        for spec, operand in zip(specs, operands)
    ]
    result = pl.pallas_call(
        kernel,
        out_shape=shapes,
        in_specs=specs,
        out_specs=[HBM] * in_hbm + [VMEM] * (len(shapes) - in_hbm),
        scratch_shapes=list(scratch),
        compiler_params=pltpu.CompilerParams(vmem_limit_bytes=mebibytes * 1024 * 1024),
        name=kernel.__name__,
    )(*operands)
    return result if len(shapes) > 1 else result[0]


def body(tokens, queries, key_rows, value_rows, cotangent, probe_shards, hess_old, shard_counts):
    length, features = tokens.shape
    half = length // 2
    packed = 2 * HEADS * HEAD
    shards = shard_counts.shape[0]
    blocks = probe_shards.shape[1] // LANES
    bf16, f32 = jnp.bfloat16, jnp.float32
    slab = pltpu.VMEM((features + SPAN, LANES), f32)
    rows = pltpu.VMEM((BLOCKS * SPAN + 8, LANES), f32)
    at = lax.axis_index("dp")
    place = jnp.stack(
        [lax.axis_index("replica"), at, at // ROW % 2, lax.axis_index("tensor") % 2]
    ).astype(jnp.int32)

    def swap_copies(array):
        return lax.ppermute(array, "replica", [(0, 1), (1, 0)])

    def swap_cores(array):
        return lax.ppermute(array, "tensor", [(one, one ^ 1) for one in range(lax.axis_size("tensor"))])

    windows, keep, to_x, to_copy = call(
        pack,
        [
            ((shards, WINDOW, LANES), bf16),
            ((length, HEADS * HEAD), bf16),
            ((half, packed + features + packed), bf16),
            ((half, features + packed), bf16),
        ],
        [SMEM] + [HBM] * 7,
        (place, shard_counts, probe_shards, tokens, queries, key_rows, value_rows, cotangent),
        12,
        (
            rows,
            pltpu.SMEM(shard_counts.shape, jnp.int32),
            pltpu.VMEM(probe_shards.shape, bf16),
            pltpu.VMEM((shards, WINDOW, LANES), bf16),
            pltpu.VMEM((HEADS, *queries.shape), bf16),
            pltpu.SemaphoreType.DMA((9,)),
        ),
        in_hbm=1,
    )
    from_x = lax.ppermute(to_x, "dp", [(one, one ^ ROW) for one in range(shards)])
    from_copy = swap_copies(to_copy)

    pieces = lax.all_to_all(windows, "dp", 0, 0)

    relayed = swap_copies(from_x[:, packed:])
    swapped = swap_cores(
        jnp.concatenate([from_x[:, packed : packed + features], from_copy[:, :features]], axis=0)
    )
    square = ((3, length, length), f32)
    update_part = ((blocks, LANES), f32)
    all_tokens, all_turned, factor, base, *parts = call(
        prepare,
        [
            ((3 * length, features), bf16),
            ((features, 3 * length), bf16),
            update_part,
            update_part,
            ((3, length, LANES), bf16),
            square,
            square,
            square,
        ],
        [SMEM, HBM, HBM, HBM],
        (place, tokens, probe_shards, hess_old, keep, from_x, from_copy, swapped),
        16,
        (
            pltpu.VMEM((3 * length, features), bf16),
            pltpu.VMEM((features, 3 * length), bf16),
            pltpu.VMEM((blocks, LANES), f32),
            pltpu.VMEM((blocks, LANES), f32),
            pltpu.VMEM(probe_shards.shape, bf16),
            pltpu.VMEM(hess_old.shape, f32),
            pltpu.SemaphoreType.DMA((7,)),
        ),
        in_hbm=4,
    )
    swapped_last = swap_cores(relayed[:, :features])
    term_windows = call(
        middle_part,
        [((shards, WINDOW, LANES), bf16)],
        [SMEM, SMEM, HBM, HBM],
        (place, shard_counts, all_tokens, all_turned, pieces, relayed, swapped_last, *parts),
        24,
        (
            slab,
            slab,
            pltpu.VMEM((features, 2 * LANES), bf16),
            pltpu.VMEM((4 * length, 2 * LANES), bf16),
            pltpu.VMEM((4 * length, features), bf16),
            pltpu.VMEM((features, 4 * length), bf16),
            pltpu.SemaphoreType.DMA((2,)),
        ),
    )
    terms = lax.all_to_all(term_windows, "dp", 0, 0)
    summed = call(add_groups, [((2 * WINDOW, LANES), f32)], [], (terms,), 8)
    sums = lax.all_gather(summed, "replica", axis=0)
    return call(
        update_shard,
        [((1, blocks * LANES), f32)],
        [SMEM, SMEM],
        (place, shard_counts, sums, factor, base),
        8,
        (rows,),
    )


def solution(mesh):
    placed = (
        P(("dp", "replica"), None),
        P(("dp", "replica"), "tensor"),
        P(("dp", "replica"), "tensor"),
        P(("dp", "replica"), "tensor"),
        P(("dp", "replica"), "tensor"),
        P("tensor", "dp"),
        P("tensor", "dp"),
        P(),
    )
    return jax.shard_map(
        body, mesh=mesh, in_specs=placed, out_specs=P("tensor", "dp"), check_vma=False
    )
```

```python
import math

import jax
import jax.numpy as jnp
from jax import lax
from jax.experimental import pallas as pl
from jax.experimental.pallas import tpu as pltpu
from jax.sharding import PartitionSpec as P

HEAD = 96
LANES = 128
decay_rate = 0.99

ROW = 8

HEADS = 4

BLOCKS = 3
WIDE = ((0, 0), (1, 0), (1, 64), (2, 64))
SLIM = ((0, 64), (0, 96), (2, 0), (2, 32))
SPAN = 64
PAIRS = SPAN // 2
QUADS = SPAN // 4
WINDOW = PAIRS + QUADS
USED = 56
HALF = LANES // 2
QUARTER = LANES // 4

VMEM = pl.BlockSpec(memory_space=pltpu.VMEM)
SMEM = pl.BlockSpec(memory_space=pltpu.SMEM)
HBM = pl.BlockSpec(memory_space=pltpu.HBM)


def lane_of(rows):
    return lax.broadcasted_iota(jnp.int32, (rows, LANES), 1)


def turn(values, lanes):
    lanes = lanes % LANES
    return values if lanes == 0 else pltpu.roll(values, lanes, 1)


def first_block(counts_ref, shard):
    return lax.fori_loop(0, shard, lambda at, total: total + counts_ref[at] // LANES, jnp.int32(0))


def by_quarter(parts):
    lane = lane_of(parts[0].shape[0])
    low = jnp.where(lane < QUARTER, parts[0], parts[1])
    high = jnp.where(lane < 3 * QUARTER, parts[2], parts[3])
    return jnp.where(lane < HALF, low, high)


def pack(
    place_ref,
    counts_hbm,
    probe_hbm,
    tokens_hbm,
    query_hbm,
    key_hbm,
    value_hbm,
    cot_hbm,
    windows_hbm,
    keep_ref,
    x_ref,
    copy_ref,
    rows,
    counts_ref,
    probe_ref,
    windows,
    held,
    sems,
):
    copy, parity, core = place_ref[0], place_ref[2], place_ref[3]
    length, features = tokens_hbm.shape
    half = length // 2
    packed = 2 * HEADS * HEAD
    shard_loads = [
        pltpu.make_async_copy(counts_hbm, counts_ref, sems.at[0]),
        pltpu.make_async_copy(probe_hbm, probe_ref, sems.at[1]),
    ]
    arrays = [held.at[at] for at in range(HEADS)]
    head_loads = [
        pltpu.make_async_copy(source, target, sems.at[2 + at])
        for at, (source, target) in enumerate(zip((query_hbm, key_hbm, value_hbm, cot_hbm), arrays))
    ]
    tokens = tokens_hbm.at[pl.ds(pl.multiple_of(core * half, half), half), :]
    token_loads = [
        pltpu.make_async_copy(tokens, x_ref.at[:, pl.ds(packed, features)], sems.at[6]),
        pltpu.make_async_copy(tokens, copy_ref.at[:, pl.ds(0, features)], sems.at[7]),
    ]
    for load in shard_loads + head_loads + token_loads:
        load.start()
    rows[...] = jnp.zeros_like(rows)
    for load in shard_loads:
        load.wait()

    shift = lax.rem(first_block(counts_ref, place_ref[1]), BLOCKS)
    for block in range(probe_ref.shape[1] // LANES):
        rows[pl.ds(shift + block, 1), :] = probe_ref[0:1, block * LANES : (block + 1) * LANES].astype(jnp.float32)

    def window(head):
        block, lane = WIDE[head]
        wide = rows[pl.ds(block, SPAN, stride=BLOCKS), :]
        pairs = jnp.where(lane_of(PAIRS) < HALF, turn(wide[:PAIRS], -lane), turn(wide[PAIRS:], HALF - lane))
        block, lane = SLIM[head]
        slim = rows[pl.ds(block, SPAN, stride=BLOCKS), :]
        quads = by_quarter(
            [turn(slim[at * QUADS : (at + 1) * QUADS], at * QUARTER - lane) for at in range(4)]
        )
        return jnp.concatenate([pairs, quads], axis=0).astype(jnp.bfloat16)

    for which in range(2):

        @pl.when(copy == which)
        def _():
            even, odd = window(2 * which), window(2 * which + 1)

            for at in range(ROW):
                windows[at] = even
                windows[ROW + at] = odd

    pair = 2 * ROW
    leaves = [
        pltpu.make_async_copy(windows, windows_hbm.at[pl.ds(at * pair, pair)], sems.at[8 + at])
        for at in range(windows_hbm.shape[0] // pair)
    ]
    for leave in leaves:
        leave.start()
    for load in head_loads:
        load.wait()

    def put(head, target_ref, start):
        for side in range(2):
            for at, ref in enumerate(arrays):
                to = start + (side * HEADS + at) * HEAD
                target_ref[:, to : to + HEAD] = ref[side * half : (side + 1) * half, head * HEAD : (head + 1) * HEAD]

    for mine in range(HEADS):

        @pl.when(2 * copy + parity == mine)
        def _():
            for at, ref in enumerate(arrays):
                keep_ref[:, at * HEAD : (at + 1) * HEAD] = ref[:, mine * HEAD : (mine + 1) * HEAD]
            put(mine ^ 1, x_ref, 0)
            put(mine ^ 3, x_ref, packed + features)
            put(mine ^ 2, copy_ref, features)

    for load in token_loads:
        load.wait()
    for leave in leaves:
        leave.wait()


def attention_part(heads):
    length = heads.shape[0]
    query, key_head, value_head, cot_head = (heads[:, at * HEAD : (at + 1) * HEAD] for at in range(HEADS))
    inv_root = 1.0 / math.sqrt(HEAD)
    causal = lax.broadcasted_iota(jnp.int32, (length, length), 0) >= lax.broadcasted_iota(
        jnp.int32, (length, length), 1
    )
    scores = inv_root * times_transposed(query, key_head)
    scores = jnp.where(causal, scores, jnp.float32(-1e30))
    expo_terms = jnp.exp(scores - jnp.max(scores, axis=1, keepdims=True))
    attn = expo_terms / jnp.sum(expo_terms, axis=1, keepdims=True)
    back = times_transposed(cot_head, value_head)
    padded_key = jnp.concatenate([key_head, jnp.zeros((length, LANES - HEAD), key_head.dtype)], axis=1)
    return padded_key, attn, back, back - jnp.sum(attn * back, axis=1, keepdims=True)


def times_transposed(left, right):
    return lax.dot_general(left, right, (((1,), (1,)), ((), ())), preferred_element_type=jnp.float32)


def join_halves(core, mine_ref, mine_at, heads_at, other_ref, other_row, tokens_ref, row):
    half, features = mine_ref.shape[0], tokens_ref.shape[1]
    side = HEADS * HEAD
    tokens_ref[pl.ds(pl.multiple_of(row + core * half, half), half), :] = mine_ref[:, mine_at : mine_at + features]
    tokens_ref[pl.ds(pl.multiple_of(row + (1 - core) * half, half), half), :] = other_ref[
        other_row : other_row + half, :
    ]
    return jnp.concatenate(
        [mine_ref[:, heads_at : heads_at + side], mine_ref[:, heads_at + side : heads_at + 2 * side]], axis=0
    )


def prepare(
    place_ref,
    tokens_hbm,
    probe_hbm,
    hess_hbm,
    keep_ref,
    x_ref,
    copy_ref,
    swapped_ref,
    tokens_out,
    turned_out,
    factor_out,
    base_out,
    key_ref,
    attn_ref,
    back_ref,
    centred_ref,
    tokens_ref,
    turned_ref,
    factor_ref,
    base_ref,
    probe_ref,
    hess_ref,
    sems,
):
    core = place_ref[3]
    length, features = tokens_hbm.shape
    packed = 2 * HEADS * HEAD
    loads = [
        pltpu.make_async_copy(tokens_hbm, tokens_ref.at[pl.ds(0, length), :], sems.at[0]),
        pltpu.make_async_copy(probe_hbm, probe_ref, sems.at[1]),
        pltpu.make_async_copy(hess_hbm, hess_ref, sems.at[2]),
    ]
    for load in loads:
        load.start()
    heads_of = [
        keep_ref[...],
        join_halves(core, x_ref, packed, 0, swapped_ref, 0, tokens_ref, length),
        join_halves(core, copy_ref, 0, features, swapped_ref, x_ref.shape[0], tokens_ref, 2 * length),
    ]
    key_ref[0], attn_ref[0], back_ref[0], centred_ref[0] = attention_part(heads_of[0])
    loads[0].wait()
    stores = [
        pltpu.make_async_copy(tokens_ref, tokens_out, sems.at[3]),
        pltpu.make_async_copy(turned_ref, turned_out, sems.at[4]),
        pltpu.make_async_copy(factor_ref, factor_out, sems.at[5]),
        pltpu.make_async_copy(base_ref, base_out, sems.at[6]),
    ]
    stores[0].start()
    turned_ref[...] = tokens_ref[...].T
    stores[1].start()
    for load in loads[1:]:
        load.wait()
    for block in range(probe_ref.shape[1] // LANES):
        lanes = slice(block * LANES, (block + 1) * LANES)
        factor_ref[block : block + 1, :] = (1.0 - decay_rate) * probe_ref[0:1, lanes].astype(jnp.float32)
        base_ref[block : block + 1, :] = decay_rate * hess_ref[0:1, lanes]
    for store in stores[2:]:
        store.start()
    for at, heads in list(enumerate(heads_of))[1:]:
        key_ref[at], attn_ref[at], back_ref[at], centred_ref[at] = attention_part(heads)
    for store in stores:
        store.wait()


def middle_part(
    place_ref,
    counts_ref,
    tokens_hbm,
    turned_hbm,
    pieces_ref,
    relay_ref,
    swapped_ref,
    key_ref,
    attn_ref,
    back_ref,
    centred_ref,
    out_ref,
    wide,
    slim,
    probe,
    spread,
    tokens,
    turned,
    sems,
):
    last = tokens_hbm.shape[0]
    load_tokens = pltpu.make_async_copy(tokens_hbm, tokens.at[pl.ds(0, last), :], sems.at[0])
    load_turned = pltpu.make_async_copy(turned_hbm, turned.at[:, pl.ds(0, last)], sems.at[1])
    load_tokens.start()
    copy, parity, core = place_ref[0], place_ref[2], place_ref[3]
    length = attn_ref.shape[1]
    features = probe.shape[0]
    shards = pieces_ref.shape[0]
    inv_root = 1.0 / math.sqrt(HEAD)
    pair_lane, quad_lane = lane_of(PAIRS), lane_of(QUADS)
    top_row = lax.broadcasted_iota(jnp.int32, (8, LANES), 0) == 0
    wide_block = (2 * copy + parity + 1) // 2
    slim_block = 2 * copy

    def place(shard, start):
        first = start // BLOCKS
        shift = start - first * BLOCKS
        piece = pieces_ref[shard].astype(jnp.float32)
        pairs, quads = piece[:PAIRS], piece[PAIRS:]
        wide_values = [jnp.where(pair_lane < HALF, pairs, 0.0), jnp.where(pair_lane < HALF, 0.0, pairs)]
        slim_values = [jnp.where(quad_lane // QUARTER == at, quads, 0.0) for at in range(4)]
        for slab, block, values in ((wide, wide_block, wide_values), (slim, slim_block, slim_values)):
            values = jnp.concatenate(values, axis=0)
            ours = jnp.logical_not(top_row & (block < shift))
            pltpu.store(slab.at[pl.ds(first, 8), :], values[:8], mask=ours)
            slab[pl.ds(first + 8, USED - 8), :] = values[8:USED]
        return start + counts_ref[shard] // LANES

    last_heads = join_halves(core, relay_ref, 0, features, swapped_ref, 0, tokens, last)
    turned[:, last:] = tokens[last:, :].T
    parts = [(key_ref[at], attn_ref[at], back_ref[at], centred_ref[at]) for at in range(key_ref.shape[0])]
    parts.append(attention_part(last_heads))
    lax.fori_loop(0, shards, place, jnp.int32(0), unroll=8)
    load_tokens.wait()
    load_turned.start()
    probe[:, :LANES] = wide[:features, :].astype(jnp.bfloat16)
    probe[:, LANES:] = slim[:features, :].astype(jnp.bfloat16)

    side = tokens.shape[0] // 2
    product = jnp.concatenate(
        [
            jnp.dot(tokens[at * side : (at + 1) * side, :], probe[...], preferred_element_type=jnp.float32)
            for at in range(2)
        ],
        axis=0,
    )
    wide_sum, slim_sum = product[:, :LANES], product[:, LANES:]
    wide_sum = wide_sum + turn(wide_sum, HALF)
    slim_sum = slim_sum + turn(slim_sum, HALF)
    slim_sum = slim_sum + turn(slim_sum, QUARTER)
    lane = lane_of(product.shape[0])
    tangent = jnp.where(
        parity == 0,
        jnp.where(lane < HALF, wide_sum, slim_sum),
        jnp.where(lane < QUARTER, slim_sum, turn(wide_sum, QUARTER)),
    ).astype(jnp.bfloat16)

    keys, attns, backs, centreds = zip(*parts)
    cuts = [slice(at * length, (at + 1) * length) for at in range(len(parts))]
    score_tangents = [inv_root * times_transposed(tangent[cut], key_head) for cut, key_head in zip(cuts, keys)]
    means = [jnp.sum(attn * score, axis=1, keepdims=True) for attn, score in zip(attns, score_tangents)]
    weights = [attn * (score - mean) for attn, score, mean in zip(attns, score_tangents, means)]
    deltas = [jnp.sum(weight * back, axis=1, keepdims=True) for weight, back in zip(weights, backs)]
    grads = [
        (weight * centred - attn * delta).astype(jnp.bfloat16)
        for weight, centred, attn, delta in zip(weights, centreds, attns, deltas)
    ]
    lane = lane_of(length)
    for cut, grad, key_head in zip(cuts, grads, keys):
        scaled = inv_root * jnp.dot(grad, key_head, preferred_element_type=jnp.float32)
        turns = [turn(scaled, at * QUARTER) for at in range(4)]
        wide_part = jnp.where(
            parity == 0,
            jnp.where(lane < HALF, scaled, turns[2]),
            jnp.where(lane < HALF, turns[3], turns[1]),
        )
        slim_part = jnp.where(
            parity == 0, by_quarter([turns[2], turns[3], scaled, turns[1]]), by_quarter(turns)
        )
        spread[cut, :LANES] = wide_part.astype(jnp.bfloat16)
        spread[cut, LANES:] = slim_part.astype(jnp.bfloat16)

    load_turned.wait()
    term = jnp.dot(turned[...], spread[...], preferred_element_type=jnp.float32)
    wide[:features, :] = term[:, :LANES]
    slim[:features, :] = term[:, LANES:]

    def cut_out(shard, start):
        first = start // BLOCKS
        pairs = jnp.where(pair_lane < HALF, wide[pl.ds(first, PAIRS), :], wide[pl.ds(first + PAIRS, PAIRS), :])
        quads = by_quarter([slim[pl.ds(first + at * QUADS, QUADS), :] for at in range(4)])
        out_ref[shard] = jnp.concatenate([pairs, quads], axis=0).astype(jnp.bfloat16)
        return start + counts_ref[shard] // LANES

    lax.fori_loop(0, shards, cut_out, jnp.int32(0), unroll=16)


def add_groups(terms_ref, out_ref):
    for parity in range(2):

        def add(at, total):
            return total + terms_ref[at // ROW * 2 * ROW + lax.rem(at, ROW) + parity * ROW].astype(jnp.float32)

        out_ref[parity * WINDOW : (parity + 1) * WINDOW, :] = lax.fori_loop(
            0, terms_ref.shape[0] // 2, add, jnp.zeros((WINDOW, LANES), jnp.float32), unroll=4
        )


def update_shard(place_ref, counts_ref, sums_ref, factor_ref, base_ref, out_ref, rows):
    shard = place_ref[1]
    shift = lax.rem(first_block(counts_ref, shard), BLOCKS)
    blocks = factor_ref.shape[0]

    def wide_part(head):
        pairs = sums_ref[head // 2, head % 2 * WINDOW : head % 2 * WINDOW + PAIRS, :]
        lane = WIDE[head][1]
        return jnp.concatenate([turn(pairs, lane - at * HALF) for at in range(2)], axis=0)

    def slim_part(head):
        quads = sums_ref[head // 2, head % 2 * WINDOW + PAIRS : (head % 2 + 1) * WINDOW, :]
        lane = SLIM[head][1]
        return jnp.concatenate([turn(quads, lane - at * QUARTER) for at in range(4)], axis=0)

    lane = lane_of(SPAN)
    rows[pl.ds(0, SPAN, stride=BLOCKS), :] = jnp.where(
        lane < HALF, wide_part(0), jnp.where(lane < 3 * QUARTER, slim_part(0), slim_part(1))
    )
    rows[pl.ds(1, SPAN, stride=BLOCKS), :] = jnp.where(lane < HALF, wide_part(1), wide_part(2))
    rows[pl.ds(2, SPAN, stride=BLOCKS), :] = jnp.where(
        lane < HALF, jnp.where(lane < QUARTER, slim_part(2), slim_part(3)), wide_part(3)
    )
    inner = lax.broadcasted_iota(jnp.int32, (blocks, LANES), 0)
    product = jnp.where(inner < counts_ref[shard] // LANES, rows[pl.ds(shift, blocks), :], 0.0)
    updated = base_ref[...] + factor_ref[...] * product
    for block in range(blocks):
        out_ref[0:1, block * LANES : (block + 1) * LANES] = updated[block : block + 1, :]


def call(kernel, outs, specs, operands, mebibytes, scratch=(), in_hbm=0):
    shapes = [
        (pltpu.HBM if at < in_hbm else jax.ShapeDtypeStruct)(shape, dtype) for at, (shape, dtype) in enumerate(outs)
    ]
    specs = specs + [VMEM] * (len(operands) - len(specs))
    operands = [
        pltpu.with_memory_space_constraint(operand, pltpu.HBM) if spec is HBM else operand
        for spec, operand in zip(specs, operands)
    ]
    result = pl.pallas_call(
        kernel,
        out_shape=shapes,
        in_specs=specs,
        out_specs=[HBM] * in_hbm + [VMEM] * (len(shapes) - in_hbm),
        scratch_shapes=list(scratch),
        compiler_params=pltpu.CompilerParams(vmem_limit_bytes=mebibytes * 1024 * 1024),
        name=kernel.__name__,
    )(*operands)
    return result if len(shapes) > 1 else result[0]


def body(tokens, queries, key_rows, value_rows, cotangent, probe_shards, hess_old, shard_counts):
    length, features = tokens.shape
    half = length // 2
    packed = 2 * HEADS * HEAD
    shards = shard_counts.shape[0]
    blocks = probe_shards.shape[1] // LANES
    bf16, f32 = jnp.bfloat16, jnp.float32
    slab = pltpu.VMEM((features + SPAN, LANES), f32)
    rows = pltpu.VMEM((BLOCKS * SPAN + 8, LANES), f32)
    at = lax.axis_index("dp")
    place = jnp.stack(
        [lax.axis_index("replica"), at, at // ROW % 2, lax.axis_index("tensor") % 2]
    ).astype(jnp.int32)

    def swap_copies(array):
        return lax.ppermute(array, "replica", [(0, 1), (1, 0)])

    def swap_cores(array):
        return lax.ppermute(array, "tensor", [(one, one ^ 1) for one in range(lax.axis_size("tensor"))])

    windows, keep, to_x, to_copy = call(
        pack,
        [
            ((shards, WINDOW, LANES), bf16),
            ((length, HEADS * HEAD), bf16),
            ((half, packed + features + packed), bf16),
            ((half, features + packed), bf16),
        ],
        [SMEM] + [HBM] * 7,
        (place, shard_counts, probe_shards, tokens, queries, key_rows, value_rows, cotangent),
        12,
        (
            rows,
            pltpu.SMEM(shard_counts.shape, jnp.int32),
            pltpu.VMEM(probe_shards.shape, bf16),
            pltpu.VMEM((2 * ROW, WINDOW, LANES), bf16),
            pltpu.VMEM((HEADS, *queries.shape), bf16),
            pltpu.SemaphoreType.DMA((8 + shards // (2 * ROW),)),
        ),
        in_hbm=1,
    )
    from_x = lax.ppermute(to_x, "dp", [(one, one ^ ROW) for one in range(shards)])
    from_copy = swap_copies(to_copy)

    pieces = lax.all_to_all(windows, "dp", 0, 0)

    relayed = swap_copies(from_x[:, packed:])
    swapped = swap_cores(
        jnp.concatenate([from_x[:, packed : packed + features], from_copy[:, :features]], axis=0)
    )
    square = ((3, length, length), f32)
    update_part = ((blocks, LANES), f32)
    all_tokens, all_turned, factor, base, *parts = call(
        prepare,
        [
            ((3 * length, features), bf16),
            ((features, 3 * length), bf16),
            update_part,
            update_part,
            ((3, length, LANES), bf16),
            square,
            square,
            square,
        ],
        [SMEM, HBM, HBM, HBM],
        (place, tokens, probe_shards, hess_old, keep, from_x, from_copy, swapped),
        16,
        (
            pltpu.VMEM((3 * length, features), bf16),
            pltpu.VMEM((features, 3 * length), bf16),
            pltpu.VMEM((blocks, LANES), f32),
            pltpu.VMEM((blocks, LANES), f32),
            pltpu.VMEM(probe_shards.shape, bf16),
            pltpu.VMEM(hess_old.shape, f32),
            pltpu.SemaphoreType.DMA((7,)),
        ),
        in_hbm=4,
    )
    swapped_last = swap_cores(relayed[:, :features])
    term_windows = call(
        middle_part,
        [((shards, WINDOW, LANES), bf16)],
        [SMEM, SMEM, HBM, HBM],
        (place, shard_counts, all_tokens, all_turned, pieces, relayed, swapped_last, *parts),
        24,
        (
            slab,
            slab,
            pltpu.VMEM((features, 2 * LANES), bf16),
            pltpu.VMEM((4 * length, 2 * LANES), bf16),
            pltpu.VMEM((4 * length, features), bf16),
            pltpu.VMEM((features, 4 * length), bf16),
            pltpu.SemaphoreType.DMA((2,)),
        ),
    )
    terms = lax.all_to_all(term_windows, "dp", 0, 0)
    summed = call(add_groups, [((2 * WINDOW, LANES), f32)], [], (terms,), 8)
    sums = lax.all_gather(summed, "replica", axis=0)
    return call(
        update_shard,
        [((1, blocks * LANES), f32)],
        [SMEM, SMEM],
        (place, shard_counts, sums, factor, base),
        8,
        (rows,),
    )


def solution(mesh):
    placed = (
        P(("dp", "replica"), None),
        P(("dp", "replica"), "tensor"),
        P(("dp", "replica"), "tensor"),
        P(("dp", "replica"), "tensor"),
        P(("dp", "replica"), "tensor"),
        P("tensor", "dp"),
        P("tensor", "dp"),
        P(),
    )
    return jax.shard_map(
        body, mesh=mesh, in_specs=placed, out_specs=P("tensor", "dp"), check_vma=False
    )
```
